128 devices in a mesh: grp: 4 (over z_lo, core), leaf: 32 (over z_hi, y, x).
Axes of the slice: x: 4, y: 4, z: 4 (z_hi: 2, z_lo: 2; z = z_hi * 2 + z_lo), core: 2. Of those that a mesh axis runs over, the one named last changes fastest.
Arguments:
- matrix: bfloat16 [32768, 32768], P('grp', 'leaf'), may hold values from -0.0625 to 0.0625
- probes: bfloat16 [32768, 512], P('leaf'), may hold values from -6 to 6
- leaf_skeleton: int32 [128, 128], P(('grp', 'leaf')), may hold values from 0 to 255, as said below
- node_skeleton: int32 [127, 128], replicated, may hold values from 0 to 255, as said below
Outputs:
- leaf_basis: float32 [32768, 128], P(('grp', 'leaf'))
- transfer: float32 [128, 256, 128], P(('grp', 'leaf'))
The draws below stay inside these ranges and needn't reach their ends.
Inputs may be any that keep to these rules, and one draw needn't show every extreme that they name: `leaf_skeleton`: each row holds 128 distinct increasing row numbers within one leaf. `node_skeleton`: each row holds 128 distinct increasing numbers into the node's stacked rows, the first child's 128 rows first.
All inputs are finite; a program needn't handle non-finite values.
Results may differ from the reference program's by a relative error of at most 0.0003.
Values sent between devices are 32-bit elements; how exact they have to be, the bound alone decides.
A program may use at most 128 MiB of HBM per device.

```python
import jax
import jax.numpy as jnp
from jax import lax

LR = 256
RANK = 128
S = 512
LEAVES = 128
N = 32768
N_LEAF = 32


def draw_leaf_skeleton(key, part):
    keys = jax.random.split(jax.random.fold_in(key, 11), LEAVES)
    picks = jax.vmap(lambda k: jnp.sort(jax.random.permutation(k, LR)[:RANK]))(keys)
    return picks.astype(jnp.int32)


def draw_node_skeleton(key, part):
    keys = jax.random.split(jax.random.fold_in(key, 23), LEAVES - 1)
    picks = jax.vmap(lambda k: jnp.sort(jax.random.permutation(k, 2 * RANK)[:RANK]))(keys)
    return picks.astype(jnp.int32)


def strengthened(values, stream_key, source, target, blocks, factor):
    def block_of(dim):
        return (jnp.arange(values.shape[dim]) // (values.shape[dim] // blocks)).reshape((-1,) + (1,) * (values.ndim - 1 - dim))

    one_side = jax.random.permutation(stream_key, blocks)[block_of(target)]
    second = (block_of(target) + blocks // 2) % blocks
    return jnp.where((block_of(source) == one_side) | (block_of(source) == second), factor * values, values)


def steps_of(key, extent, cuts, low, top_value):
    level, own = 1.0, jax.random.fold_in(key, 6)
    for dim, shards_of in cuts:
        steps = jnp.exp(jax.random.uniform(jax.random.fold_in(own, dim), (shards_of,), jnp.float32, low / len(cuts), top_value / len(cuts)))
        level = level * jnp.repeat(steps, extent[dim] // shards_of).reshape([-1 if axis == dim else 1 for axis in range(len(extent))])
    return level


def gaussian(own_key, extent, deviation, limit, cuts=(), held_as=jnp.bfloat16):
    values = deviation * jax.random.normal(own_key, extent, jnp.float32)
    if cuts:
        values = values * steps_of(own_key, extent, cuts, -0.22, 0.18)
    return jnp.clip(values, -limit, limit).astype(held_as)


def bell_draw_with(own_key, dims, width, limit, cuts, heavy, kind=jnp.bfloat16):
    result = width * jax.random.normal(own_key, dims, jnp.float32)
    if cuts:
        result = result * steps_of(own_key, dims, cuts, -0.22, 0.18)
    return jnp.clip(strengthened(result, jax.random.fold_in(own_key, 3), *heavy), -limit, limit).astype(kind)


def setup_inputs(seed: int = 0) -> dict:
    key_list = jax.random.split(jax.random.key(seed), 5)
    return {
        "matrix": bell_draw_with(key_list[0], (N, N), N ** -0.5, 0.0625, ((0, 4), (1, 32)), (1, 0, 32, 2.75)),
        "probes": gaussian(key_list[1], (N, S), 1.0, 6.0, ((0, 32),)),
        "leaf_skeleton": draw_leaf_skeleton(jax.random.fold_in(key_list[4], 71), 0),
        "node_skeleton": draw_node_skeleton(jax.random.fold_in(key_list[4], 71), 0),
    }


def node_bases(stacked, picked):
    rows = jnp.take_along_axis(stacked, picked[:, :, None], axis=1)
    gram = jnp.einsum('nks,nls->nkl', rows, rows, precision=lax.Precision.HIGHEST)
    cross = jnp.einsum('nks,nis->nki', rows, stacked, precision=lax.Precision.HIGHEST)
    factor = jnp.linalg.cholesky(gram)
    first = lax.linalg.triangular_solve(factor, cross, left_side=True, lower=True)
    solved = lax.linalg.triangular_solve(factor, first, left_side=True, lower=True, transpose_a=True)
    return (jnp.swapaxes(solved, 1, 2), rows)

def reference(matrix, probes, leaf_skeleton, node_skeleton):
    cols = N // N_LEAF
    row_leaf = jnp.arange(N, dtype=jnp.int32) // LR

    def add_block(block_index, total):
        start = (block_index * cols).astype(jnp.int32)
        block = lax.dynamic_slice_in_dim(matrix, start, cols, 1)
        col_leaf = (start + jnp.arange(cols, dtype=jnp.int32)) // LR
        keep = row_leaf[:, None] != col_leaf[None, :]
        block = jnp.where(keep, block, jnp.zeros((), matrix.dtype))
        probe_rows = lax.dynamic_slice_in_dim(probes, start, cols, 0)
        part = jnp.dot(block.astype(jnp.float32), probe_rows.astype(jnp.float32), preferred_element_type=jnp.float32)
        return total + part
    samples = lax.fori_loop(jnp.int32(0), jnp.int32(N_LEAF), add_block, jnp.zeros((N, S), jnp.float32))
    leaves = samples.reshape(LEAVES, LR, S)
    basis, carried = node_bases(leaves, leaf_skeleton)
    leaf_basis = basis.reshape(N, RANK)
    levels = int(LEAVES).bit_length() - 1
    uppers = []
    offset = 0
    count = LEAVES
    for level in range(levels):
        count = count // 2
        stacked = carried.reshape(count, 2 * RANK, S)
        picked = node_skeleton[offset:offset + count]
        upper, carried = node_bases(stacked, picked)
        uppers.append(upper)
        offset = offset + count
    table = []
    for device in range(LEAVES):
        if device == 0:
            level = levels
        else:
            level = (device & -device).bit_length()
        table.append(uppers[level - 1][device >> level])
    return (leaf_basis, jnp.stack(table))
```

```python
import jax
import jax.numpy as jnp
from jax import lax
from jax.sharding import PartitionSpec as P


def from_partner(value, axis, stride):
    mask = 2**stride
    pairs = [(source, source ^ mask) for source in range(lax.axis_size(axis))]
    return lax.ppermute(value, axis, pairs)


def node_bases(stacked, picked):
    rows = jnp.take_along_axis(stacked, picked[:, :, None], axis=1)
    gram = jnp.einsum("nks,nls->nkl", rows, rows, precision=lax.Precision.HIGHEST)
    cross = jnp.einsum("nks,nis->nki", rows, stacked, precision=lax.Precision.HIGHEST)
    factor = jnp.linalg.cholesky(gram)
    first = lax.linalg.triangular_solve(factor, cross, left_side=True, lower=True)
    solved = lax.linalg.triangular_solve(
        factor, first, left_side=True, lower=True, transpose_a=True
    )
    return jnp.swapaxes(solved, 1, 2)


def on_device(matrix, probes, leaf_skeleton, node_skeleton):
    n_grp = lax.axis_size("grp")
    n_leaf = lax.axis_size("leaf")
    grp_pos = lax.axis_index("grp")
    leaf_pos = lax.axis_index("leaf")
    device = grp_pos * n_leaf + leaf_pos
    row_count, col_count = matrix.shape
    leaf_rows = row_count // n_leaf
    rank = leaf_skeleton.shape[1]
    all_leaves = n_grp * n_leaf
    leaf_bits = n_leaf.bit_length() - 1
    grp_bits = n_grp.bit_length() - 1
    levels = leaf_bits + grp_bits
    row_leaf = grp_pos * n_leaf + jnp.arange(row_count, dtype=jnp.int32) // leaf_rows
    col_leaf = (leaf_pos * col_count + jnp.arange(col_count, dtype=jnp.int32)) // leaf_rows
    block = jnp.where(
        row_leaf[:, None] != col_leaf[None, :], matrix, jnp.zeros((), matrix.dtype)
    )
    samples_mine = lax.psum_scatter(
        jnp.dot(block, probes, preferred_element_type=jnp.float32),
        "leaf",
        scatter_dimension=0,
        tiled=True,
    )
    current = jnp.take(samples_mine, leaf_skeleton[0], axis=0)
    mine = jnp.zeros((2 * rank, samples_mine.shape[1]), jnp.float32)
    mine_picked = leaf_skeleton[0]
    offset = 0
    for level in range(1, levels + 1):
        if level <= leaf_bits:
            bit = leaf_pos >> (level - 1) & 1
            partner = from_partner(current, "leaf", level - 1)
        else:
            bit = grp_pos >> (level - 1 - leaf_bits) & 1
            partner = from_partner(current, "grp", level - 1 - leaf_bits)
        lower = jnp.where(bit == 1, partner, current)
        upper = jnp.where(bit == 1, current, partner)
        stacked = jnp.concatenate([lower, upper], axis=0)
        picked = node_skeleton[offset + (device >> level)]
        offset += all_leaves >> level
        select = (device % (1 << level) == 1 << level - 1) | (device == 0) & (level == levels)
        mine = jnp.where(select, stacked, mine)
        mine_picked = jnp.where(select, picked, mine_picked)
        if level < levels:
            current = jnp.take(stacked, picked, axis=0)
    bases = node_bases(
        jnp.stack([samples_mine, mine]), jnp.stack([leaf_skeleton[0], mine_picked])
    )
    return (bases[0], bases[1:])


def solution(mesh):
    return jax.shard_map(
        on_device,
        mesh=mesh,
        in_specs=(P("grp", "leaf"), P("leaf", None), P(("grp", "leaf"), None), P()),
        out_specs=(P(("grp", "leaf"), None), P(("grp", "leaf"), None, None)),
        check_vma=False,
    )
```

```python
import jax
import jax.numpy as jnp
from jax import lax
from jax.experimental import pallas as pl
from jax.experimental.pallas import tpu as pltpu
from jax.sharding import PartitionSpec as P

NX, NY, NZ = 4, 4, 2
LR = 256
RANK = 128
HALF = 256
SLOTS = 8
CHUNKS = ((0, 128), (128, 128))
F32 = jnp.float32
BF16 = jnp.bfloat16
ORDER = (
    [(2, 0), (2, 1), (2, 2), (2, 3)]
    + [(0, 2), (1, 2), (3, 2)]
    + [(1, 0), (1, 1), (1, 3)]
    + [(3, 0), (3, 1), (3, 3)]
    + [(0, 1), (0, 3), (0, 0)]
)
OPP_R, OPP_L, NEAR_RA, NEAR_RB, NEAR_LA, NEAR_LB = range(6)
PASS = 6
Z_COPY = 2 * PASS
N_COPY = 2 * PASS + 1


def mod4(v):
    return lax.rem(v + 4, 4)


class Half:
    def __init__(self, part, bufs, zbuf, send, recv, rows, first, second, zh, dev):
        self.part, self.bufs, self.zbuf = part, bufs, zbuf
        self.send, self.recv = send, recv
        self.rows = rows
        self.axes = (first, second)
        self.zh = zh
        self.dev = dev
        self.started = []

    def block(self, phase, index):
        if phase == 0:
            return self.part.at[index]
        return self.part.at[self.axes[0][1], index]

    def copy(self, phase, kind):
        name, me = self.axes[phase]
        half = self.rows // 2
        opp, near_r, near_l = self.bufs[phase]
        lo, hi = pl.ds(0, half), pl.ds(half, half)
        lead = (slice(None),) * (2 if phase == 0 else 1)
        right, left = mod4(me + 1), mod4(me - 1)
        index, rows, dst, to = {
            OPP_R: (mod4(me + 2), lo, opp.at[0], right),
            OPP_L: (mod4(me + 2), hi, opp.at[1], left),
            NEAR_RA: (right, lo, near_r.at[(*lead, lo)], right),
            NEAR_RB: (right, hi, near_r.at[(*lead, hi)], right),
            NEAR_LA: (left, lo, near_l.at[(*lead, lo)], left),
            NEAR_LB: (left, hi, near_l.at[(*lead, hi)], left),
        }[kind]
        slot = phase * PASS + kind
        return pltpu.make_async_remote_copy(
            src_ref=self.block(phase, index).at[(*lead, rows)],
            dst_ref=dst,
            send_sem=self.send.at[slot],
            recv_sem=self.recv.at[slot],
            device_id=self.dev(**{name: to}),
            device_id_type=pl.DeviceIdType.MESH,
        )

    def start(self, phase, *kinds):
        for kind in kinds:
            copy = self.copy(phase, kind)
            copy.start()
            self.started.append(copy)

    def wait(self, phase, kind):
        self.copy(phase, kind).wait_recv()

    def relay(self, phase):
        me = self.axes[phase][1]
        half = self.rows // 2
        opp = self.bufs[phase][0]
        for kind, side, index, row, on in (
            (OPP_R, 0, mod4(me + 1), 0, NEAR_RA),
            (OPP_L, 1, mod4(me - 1), half, NEAR_LB),
        ):
            self.wait(phase, kind)
            self.add(phase, index, row, half, (opp.at[side],), 0)
            self.start(phase, on)

    def gather(self, phase):
        me = self.axes[phase][1]
        for kind in (NEAR_RB, NEAR_LA, NEAR_RA, NEAR_LB):
            self.wait(phase, kind)
        self.add(phase, me, 0, self.rows, self.bufs[phase][1:], 0)

    def add(self, phase, index, row, count, terms, term_row):
        target = self.block(phase, index)
        rows, term_rows = pl.ds(row, count), pl.ds(term_row, count)
        if phase == 0:

            def step(i, carry):
                at = (i // NZ, lax.rem(i, NZ))
                value = target[(*at, rows)]
                for term in terms:
                    value = value + term[(*at, term_rows)]
                target[(*at, rows)] = value
                return carry

            lax.fori_loop(0, 4 * NZ, step, 0)
        else:
            for z in range(NZ):
                value = target[z, rows]
                for term in terms:
                    value = value + term[z, term_rows]
                target[z, rows] = value

    def z_copy(self):
        return pltpu.make_async_remote_copy(
            src_ref=self.part.at[self.axes[0][1], self.axes[1][1], 1 - self.zh],
            dst_ref=self.zbuf,
            send_sem=self.send.at[Z_COPY],
            recv_sem=self.recv.at[Z_COPY],
            device_id=self.dev(z=1 - self.zh),
            device_id_type=pl.DeviceIdType.MESH,
        )

    def z_start(self):
        copy = self.z_copy()
        copy.start()
        self.started.append(copy)

    def z_finish(self):
        self.z_copy().wait_recv()
        return self.part[self.axes[0][1], self.axes[1][1], self.zh] + self.zbuf[...]


def leaf_order(skel):
    hit = (lax.broadcasted_iota(jnp.int32, (LR, RANK), 0) == skel).astype(F32).astype(BF16)
    picked = lax.dot_general(
        jnp.ones((8, RANK), BF16), hit, (((1,), (1,)), ((), ())), preferred_element_type=F32
    )
    before = (
        (
            lax.broadcasted_iota(jnp.int32, (LR, LR), 0)
            < lax.broadcasted_iota(jnp.int32, (LR, LR), 1)
        )
        .astype(F32)
        .astype(BF16)
    )
    count = jnp.dot(picked.astype(BF16), before, preferred_element_type=F32)
    lane = lax.broadcasted_iota(jnp.int32, (8, LR), 1).astype(F32)
    place = jnp.where(picked > 0.5, count, RANK + lane - count)
    return place[0:1]


def kernel(
    matrix,
    probes,
    skel,
    out,
    order_out,
    slots,
    permuted,
    places,
    in_sem,
    place_send,
    place_recv,
    send,
    recv,
    *rest,
):
    leaf = lax.axis_index("leaf")
    grp = lax.axis_index("grp")
    x = lax.rem(leaf, NX)
    y = lax.rem(leaf // NX, NY)
    zh = leaf // (NX * NY)

    def dev(x=x, y=y, z=zh):
        return {"leaf": (z * NY + y) * NX + x}

    barrier = pltpu.get_barrier_semaphore()
    peers = [dev(x=mod4(x + k)) for k in (1, 2, 3)]
    peers += [dev(y=mod4(y + k)) for k in (1, 2, 3)]
    peers += [dev(z=1 - zh)]
    for peer in peers:
        pl.semaphore_signal(barrier, 1, device_id=peer, device_id_type=pl.DeviceIdType.MESH)

    def place_of(t):
        pair = t // NZ
        i = sum(jnp.where(pair == k, o[0], 0) for k, o in enumerate(ORDER))
        j = sum(jnp.where(pair == k, o[1], 0) for k, o in enumerate(ORDER))
        return mod4(x + i), mod4(y + j), lax.rem(t, NZ)

    def load(t):
        xd, yd, zd = place_of(t)
        dest = (zd * NY + yd) * NX + xd
        slot = lax.rem(t, SLOTS)
        return pltpu.make_async_copy(
            matrix.at[pl.ds(pl.multiple_of(dest * LR, LR), LR), :],
            slots.at[slot],
            in_sem.at[slot],
        )

    def prefetch(t, carry):
        load(t).start()
        return carry

    lax.fori_loop(0, SLOTS, prefetch, 0)

    place = leaf_order(skel[...])
    order_out[...] = place
    places[zh, y, x] = place
    pl.semaphore_wait(barrier, len(peers))

    def share(src, slot, peer):
        return pltpu.make_async_remote_copy(
            src_ref=src,
            dst_ref=src,
            send_sem=place_send.at[slot],
            recv_sem=place_recv.at[slot],
            device_id=peer,
            device_id_type=pl.DeviceIdType.MESH,
        )

    shared = []
    for base, src, targets in (
        (0, places.at[zh, y, x], peers[0:3]),
        (3, places.at[zh, y], peers[3:6]),
        (6, places.at[zh], peers[6:7]),
    ):
        stage = [share(src, base + k, peer) for k, peer in enumerate(targets)]
        for copy in stage:
            copy.start()
        for copy in stage:
            copy.wait_recv()
        shared += stage

    halves = []
    rest = list(rest)
    parts = []
    for c, (_, rows) in enumerate(CHUNKS):
        pair = []
        for h in range(2):
            part, o1, r1, l1, o2, r2, l2, zb = rest[:8]
            rest = rest[8:]
            first, second = (("x", x), ("y", y)) if h == 0 else (("y", y), ("x", x))
            pair.append(
                Half(
                    part,
                    ((o1, r1, l1), (o2, r2, l2)),
                    zb,
                    send.at[c, h],
                    recv.at[c, h],
                    rows,
                    first,
                    second,
                    zh,
                    dev,
                )
            )
        halves.append(pair)

    def multiply(t, carry):
        xd, yd, zd = place_of(t)
        dest = (zd * NY + yd) * NX + xd
        slot = lax.rem(t, SLOTS)
        load(t).wait()
        rows_iota = lax.broadcasted_iota(jnp.int32, (LR, LR), 0).astype(F32)
        pick = (rows_iota == places[zd, yd, xd]).astype(F32).astype(BF16)
        for b in range(probes.shape[0] // LR):
            cols = pl.ds(b * LR, LR)
            moved = jnp.dot(pick, slots[slot, :, cols], preferred_element_type=F32)
            own = leaf * (probes.shape[0] // LR) + b == grp * (NX * NY * NZ) + dest
            permuted[:, cols] = jnp.where(own, 0.0, moved).astype(BF16)
        for h in range(2):
            product = jnp.dot(
                permuted[...], probes[:, pl.ds(h * HALF, HALF)], preferred_element_type=F32
            )
            for c, (row, rows) in enumerate(CHUNKS):
                at = (xd, yd, zd) if h == 0 else (yd, xd, zd)
                halves[c][h].part[at] = product[row : row + rows]

        @pl.when(t + SLOTS < NX * NY * NZ)
        def _():
            load(t + SLOTS).start()

        return carry

    a, b = halves
    lax.fori_loop(0, 8, multiply, 0)
    a[0].start(0, OPP_R, OPP_L)
    lax.fori_loop(8, 14, multiply, 0)
    a[1].start(0, OPP_R, OPP_L)
    lax.fori_loop(14, 20, multiply, 0)
    a[0].start(0, NEAR_RB)
    lax.fori_loop(20, 26, multiply, 0)
    a[0].start(0, NEAR_LA)
    lax.fori_loop(26, 32, multiply, 0)
    a[1].start(0, NEAR_RB, NEAR_LA)
    for h in range(2):
        a[h].relay(0)
    for h in range(2):
        b[h].start(0, OPP_R, OPP_L)
    for h in range(2):
        a[h].gather(0)
        a[h].start(1, OPP_R, OPP_L, NEAR_RB, NEAR_LA)
    for h in range(2):
        b[h].start(0, NEAR_RB, NEAR_LA)
    for h in range(2):
        a[h].relay(1)
    for h in range(2):
        b[h].relay(0)
    for h in range(2):
        a[h].gather(1)
        a[h].z_start()
    for h in range(2):
        out[pl.ds(0, 128), pl.ds(h * HALF, HALF)] = a[h].z_finish()
    for h in range(2):
        b[h].gather(0)
        b[h].start(1, OPP_R, OPP_L, NEAR_RB, NEAR_LA)
    for h in range(2):
        b[h].relay(1)
    for h in range(2):
        b[h].gather(1)
        b[h].z_start()
    for h in range(2):
        out[pl.ds(128, 128), pl.ds(h * HALF, HALF)] = b[h].z_finish()
    for copy in shared:
        copy.wait_send()
    for pair in halves:
        for half in pair:
            for copy in half.started:
                copy.wait_send()


def reduced_rows(matrix, probes, skel):
    depth = probes.shape[0]
    scratch = [
        pltpu.VMEM((SLOTS, LR, depth), BF16),
        pltpu.VMEM((LR, depth), BF16),
        pltpu.VMEM((NZ, NY, NX, 1, LR), F32),
        pltpu.SemaphoreType.DMA((SLOTS,)),
        pltpu.SemaphoreType.DMA((7,)),
        pltpu.SemaphoreType.DMA((7,)),
        pltpu.SemaphoreType.DMA((len(CHUNKS), 2, N_COPY)),
        pltpu.SemaphoreType.DMA((len(CHUNKS), 2, N_COPY)),
    ]
    for _, rows in CHUNKS:
        for _ in range(2):
            scratch += [
                pltpu.VMEM((4, 4, NZ, rows, HALF), F32),
                pltpu.VMEM((2, 4, NZ, rows // 2, HALF), F32),
                pltpu.VMEM((4, NZ, rows, HALF), F32),
                pltpu.VMEM((4, NZ, rows, HALF), F32),
                pltpu.VMEM((2, NZ, rows // 2, HALF), F32),
                pltpu.VMEM((NZ, rows, HALF), F32),
                pltpu.VMEM((NZ, rows, HALF), F32),
                pltpu.VMEM((rows, HALF), F32),
            ]
    vmem = pl.BlockSpec(memory_space=pltpu.VMEM)
    return pl.pallas_call(
        kernel,
        out_shape=(
            jax.ShapeDtypeStruct((LR, probes.shape[1]), F32),
            jax.ShapeDtypeStruct((1, LR), F32),
        ),
        in_specs=[pl.BlockSpec(memory_space=pl.ANY), vmem, vmem],
        out_specs=(vmem, vmem),
        scratch_shapes=scratch,
        compiler_params=pltpu.CompilerParams(
            collective_id=0, has_side_effects=True, vmem_limit_bytes=56 * 2**20
        ),
        name="reduced_rows",
    )(matrix, probes, skel)


def from_partner(value, axis, stride):
    mask = 2**stride
    pairs = [(source, source ^ mask) for source in range(lax.axis_size(axis))]
    return lax.ppermute(value, axis, pairs)


def node_bases(stacked, picked):
    rows = jnp.take_along_axis(stacked, picked[:, :, None], axis=1)
    gram = jnp.einsum("nks,nls->nkl", rows, rows, precision=lax.Precision.HIGHEST)
    cross = jnp.einsum("nks,nis->nki", rows, stacked, precision=lax.Precision.HIGHEST)
    factor = jnp.linalg.cholesky(gram)
    first = lax.linalg.triangular_solve(factor, cross, left_side=True, lower=True)
    solved = lax.linalg.triangular_solve(
        factor, first, left_side=True, lower=True, transpose_a=True
    )
    return jnp.swapaxes(solved, 1, 2)


def on_device(matrix, probes, leaf_skeleton, node_skeleton):
    n_grp = lax.axis_size("grp")
    n_leaf = lax.axis_size("leaf")
    grp_pos = lax.axis_index("grp")
    leaf_pos = lax.axis_index("leaf")
    device = grp_pos * n_leaf + leaf_pos
    rank = leaf_skeleton.shape[1]
    all_leaves = n_grp * n_leaf
    leaf_bits = n_leaf.bit_length() - 1
    grp_bits = n_grp.bit_length() - 1
    levels = leaf_bits + grp_bits
    moved, place = reduced_rows(matrix, probes, leaf_skeleton)
    samples_mine = jnp.take(moved, place[0].astype(jnp.int32), axis=0)
    current = moved[:rank]
    mine = jnp.zeros((2 * rank, samples_mine.shape[1]), jnp.float32)
    mine_picked = leaf_skeleton[0]
    offset = 0
    for level in range(1, levels + 1):
        if level <= leaf_bits:
            bit = leaf_pos >> (level - 1) & 1
            partner = from_partner(current, "leaf", level - 1)
        else:
            bit = grp_pos >> (level - 1 - leaf_bits) & 1
            partner = from_partner(current, "grp", level - 1 - leaf_bits)
        lower = jnp.where(bit == 1, partner, current)
        upper = jnp.where(bit == 1, current, partner)
        stacked = jnp.concatenate([lower, upper], axis=0)
        picked = node_skeleton[offset + (device >> level)]
        offset += all_leaves >> level
        select = (device % (1 << level) == 1 << level - 1) | (device == 0) & (level == levels)
        mine = jnp.where(select, stacked, mine)
        mine_picked = jnp.where(select, picked, mine_picked)
        if level < levels:
            current = jnp.take(stacked, picked, axis=0)
    bases = node_bases(
        jnp.stack([samples_mine, mine]), jnp.stack([leaf_skeleton[0], mine_picked])
    )
    return (bases[0], bases[1:])


def solution(mesh):
    return jax.shard_map(
        on_device,
        mesh=mesh,
        in_specs=(P("grp", "leaf"), P("leaf", None), P(("grp", "leaf"), None), P()),
        out_specs=(P(("grp", "leaf"), None), P(("grp", "leaf"), None, None)),
        check_vma=False,
    )
```

```python
import jax
import jax.numpy as jnp
from jax import lax
from jax.experimental import pallas as pl
from jax.experimental.pallas import tpu as pltpu
from jax.sharding import PartitionSpec as P

NX, NY, NZ = 4, 4, 2
LR = 256
RANK = 128
HALF = 256
SLOTS = 8
CHUNKS = ((0, 128), (128, 128))
PIECES = 4
PIECE = 128
LEVELS = 7
GROUP = NX * NY * NZ
LEAVES = 128
PANEL = 16
HIGHEST = lax.Precision.HIGHEST
F32 = jnp.float32
BF16 = jnp.bfloat16
ORDER = (
    [(2, 0), (2, 1), (2, 2), (2, 3)]
    + [(0, 2), (1, 2), (3, 2)]
    + [(1, 0), (1, 1), (1, 3)]
    + [(3, 0), (3, 1), (3, 3)]
    + [(0, 1), (0, 3), (0, 0)]
)
OPP_R, OPP_L, NEAR_RA, NEAR_RB, NEAR_LA, NEAR_LB = range(6)
PASS = 6
Z_COPY = 2 * PASS
N_COPY = 2 * PASS + 1


def mod4(v):
    return lax.rem(v + 4, 4)


class Half:
    def __init__(self, part, bufs, zbuf, send, recv, rows, first, second, zh, dev):
        self.part, self.bufs, self.zbuf = part, bufs, zbuf
        self.send, self.recv = send, recv
        self.rows = rows
        self.axes = (first, second)
        self.zh = zh
        self.dev = dev
        self.started = []

    def block(self, phase, index):
        if phase == 0:
            return self.part.at[index]
        return self.part.at[self.axes[0][1], index]

    def copy(self, phase, kind):
        name, me = self.axes[phase]
        half = self.rows // 2
        opp, near_r, near_l = self.bufs[phase]
        lo, hi = pl.ds(0, half), pl.ds(half, half)
        lead = (slice(None),) * (2 if phase == 0 else 1)
        right, left = mod4(me + 1), mod4(me - 1)
        index, rows, dst, to = {
            OPP_R: (mod4(me + 2), lo, opp.at[0], right),
            OPP_L: (mod4(me + 2), hi, opp.at[1], left),
            NEAR_RA: (right, lo, near_r.at[(*lead, lo)], right),
            NEAR_RB: (right, hi, near_r.at[(*lead, hi)], right),
            NEAR_LA: (left, lo, near_l.at[(*lead, lo)], left),
            NEAR_LB: (left, hi, near_l.at[(*lead, hi)], left),
        }[kind]
        slot = phase * PASS + kind
        return pltpu.make_async_remote_copy(
            src_ref=self.block(phase, index).at[(*lead, rows)],
            dst_ref=dst,
            send_sem=self.send.at[slot],
            recv_sem=self.recv.at[slot],
            device_id=self.dev(**{name: to}),
            device_id_type=pl.DeviceIdType.MESH,
        )

    def start(self, phase, *kinds):
        for kind in kinds:
            copy = self.copy(phase, kind)
            copy.start()
            self.started.append(copy)

    def wait(self, phase, kind):
        self.copy(phase, kind).wait_recv()

    def relay(self, phase):
        me = self.axes[phase][1]
        half = self.rows // 2
        opp = self.bufs[phase][0]
        for kind, side, index, row, on in (
            (OPP_R, 0, mod4(me + 1), 0, NEAR_RA),
            (OPP_L, 1, mod4(me - 1), half, NEAR_LB),
        ):
            self.wait(phase, kind)
            self.add(phase, index, row, half, (opp.at[side],), 0)
            self.start(phase, on)

    def gather(self, phase):
        me = self.axes[phase][1]
        for kind in (NEAR_RB, NEAR_LA, NEAR_RA, NEAR_LB):
            self.wait(phase, kind)
        self.add(phase, me, 0, self.rows, self.bufs[phase][1:], 0)

    def add(self, phase, index, row, count, terms, term_row):
        target = self.block(phase, index)
        rows, term_rows = pl.ds(row, count), pl.ds(term_row, count)
        if phase == 0:

            def step(i, carry):
                at = (i // NZ, lax.rem(i, NZ))
                value = target[(*at, rows)]
                for term in terms:
                    value = value + term[(*at, term_rows)]
                target[(*at, rows)] = value
                return carry

            lax.fori_loop(0, 4 * NZ, step, 0)
        else:
            for z in range(NZ):
                value = target[z, rows]
                for term in terms:
                    value = value + term[z, term_rows]
                target[z, rows] = value

    def z_copy(self):
        return pltpu.make_async_remote_copy(
            src_ref=self.part.at[self.axes[0][1], self.axes[1][1], 1 - self.zh],
            dst_ref=self.zbuf,
            send_sem=self.send.at[Z_COPY],
            recv_sem=self.recv.at[Z_COPY],
            device_id=self.dev(z=1 - self.zh),
            device_id_type=pl.DeviceIdType.MESH,
        )

    def z_start(self):
        copy = self.z_copy()
        copy.start()
        self.started.append(copy)

    def z_finish(self):
        self.z_copy().wait_recv()
        return self.part[self.axes[0][1], self.axes[1][1], self.zh] + self.zbuf[...]


def leaf_order(skel):
    hit = (lax.broadcasted_iota(jnp.int32, (LR, RANK), 0) == skel).astype(F32).astype(BF16)
    picked = lax.dot_general(
        jnp.ones((8, RANK), BF16), hit, (((1,), (1,)), ((), ())), preferred_element_type=F32
    )
    before = (
        (
            lax.broadcasted_iota(jnp.int32, (LR, LR), 0)
            < lax.broadcasted_iota(jnp.int32, (LR, LR), 1)
        )
        .astype(F32)
        .astype(BF16)
    )
    count = jnp.dot(picked.astype(BF16), before, preferred_element_type=F32)
    lane = lax.broadcasted_iota(jnp.int32, (8, LR), 1).astype(F32)
    place = jnp.where(picked > 0.5, count, RANK + lane - count)
    return place[0:1]


def selection(place):
    return (lax.broadcasted_iota(jnp.int32, (LR, LR), 0).astype(F32) == place).astype(F32)


def select(pick, value):
    total = 0.0
    for _ in range(3):
        term = value.astype(BF16)
        total = total + jnp.dot(pick, term, preferred_element_type=F32)
        value = value - term.astype(F32)
    return total


def times_transposed(a, b):
    return lax.dot_general(
        a, b, (((1,), (1,)), ((), ())), precision=HIGHEST, preferred_element_type=F32
    )


def eliminate(panels):
    lane = lax.broadcasted_iota(jnp.int32, panels[0].shape, 1)
    sub = lax.broadcasted_iota(jnp.int32, panels[0].shape, 0)
    for k in range(PANEL):
        done = []
        for p in panels:
            row = jnp.where(lane[0:1] == k, 1.0, p[k : k + 1]) * (1.0 / p[k : k + 1, k : k + 1])
            rest = jnp.where(lane == k, 0.0, p) - p[:, k : k + 1] * row
            done.append(jnp.where(sub == k, row, rest))
        panels = done
    return panels


def inverses(grams):
    def body(_, grams):
        panels = eliminate([g[:PANEL] for g in grams])
        done = []
        for g, p in zip(grams, panels):
            rest = g[PANEL:]
            lane = lax.broadcasted_iota(jnp.int32, rest.shape, 1)
            rest = jnp.where(lane < PANEL, 0.0, rest) - jnp.dot(
                rest[:, :PANEL], p, precision=HIGHEST, preferred_element_type=F32
            )
            done.append(pltpu.roll(jnp.concatenate([rest, p], 0), RANK - PANEL, 1))
        return tuple(done)

    return lax.fori_loop(0, RANK // PANEL, body, tuple(grams))


def kernel(
    matrix,
    probes,
    skel,
    node_skel,
    leaf_out,
    node_out,
    slots,
    permuted,
    places,
    leaf_rows,
    node_rows,
    stack,
    unpick,
    weights,
    in_sem,
    place_send,
    place_recv,
    tree_send,
    tree_recv,
    send,
    recv,
    *rest,
):
    leaf = lax.axis_index("leaf")
    grp = lax.axis_index("grp")
    x = lax.rem(leaf, NX)
    y = lax.rem(leaf // NX, NY)
    zh = leaf // (NX * NY)

    def dev(x=x, y=y, z=zh):
        return {"leaf": (z * NY + y) * NX + x}

    barrier = pltpu.get_barrier_semaphore()
    peers = [dev(x=mod4(x + k)) for k in (1, 2, 3)]
    peers += [dev(y=mod4(y + k)) for k in (1, 2, 3)]
    peers += [dev(z=1 - zh)]
    for peer in peers:
        pl.semaphore_signal(barrier, 1, device_id=peer, device_id_type=pl.DeviceIdType.MESH)

    me = grp * GROUP + leaf
    odd = lax.rem(me, 2) == 1
    level = jnp.int32(1)
    for k in range(1, LEVELS):
        level = jnp.where(lax.rem(me, 2**k) == 0, k + 1, level)
    step = sum(jnp.where(level == k, 2 ** (k - 1), 0) for k in range(1, LEVELS + 1))
    node = sum(
        jnp.where(level == k, LEAVES - (LEAVES >> (k - 1)) + me // 2**k, 0)
        for k in range(1, LEVELS + 1)
    )
    side = lax.rem(me // (2 * step), 2)
    parent = jnp.where(side == 0, me + step, me - step)
    top = me == 0

    def device_of(number):
        number = lax.rem(number + LEAVES, LEAVES)
        return {"grp": number // GROUP, "leaf": lax.rem(number, GROUP)}

    def greet(number):
        pl.semaphore_signal(
            barrier, 1, device_id=device_of(number), device_id_type=pl.DeviceIdType.MESH
        )

    @pl.when(odd)
    def _():
        greet(me - 1)

    @pl.when(jnp.logical_not(odd))
    def _():
        greet(jnp.where(top, LEAVES // 4, me - step // 2))
        greet(jnp.where(top, 3 * LEAVES // 4, me + step // 2))

    greeted = len(peers) + jnp.where(odd, 0, 1)
    greeted = greeted + jnp.where(level < LEVELS, 1, 0) + jnp.where(level == LEVELS - 1, 1, 0)

    def place_of(t):
        pair = t // NZ
        i = sum(jnp.where(pair == k, o[0], 0) for k, o in enumerate(ORDER))
        j = sum(jnp.where(pair == k, o[1], 0) for k, o in enumerate(ORDER))
        return mod4(x + i), mod4(y + j), lax.rem(t, NZ)

    def load(t):
        xd, yd, zd = place_of(t)
        dest = (zd * NY + yd) * NX + xd
        slot = lax.rem(t, SLOTS)
        return pltpu.make_async_copy(
            matrix.at[pl.ds(pl.multiple_of(dest * LR, LR), LR), :],
            slots.at[slot],
            in_sem.at[slot],
        )

    def prefetch(t, carry):
        load(t).start()
        return carry

    lax.fori_loop(0, SLOTS, prefetch, 0)

    place = leaf_order(skel[...])
    places[zh, y, x] = place
    node_pick = selection(leaf_order(node_skel[pl.ds(node, 1), :]))[:RANK].astype(BF16)
    unpick[...] = selection(place).T
    pl.semaphore_wait(barrier, greeted)

    def share(src, slot, peer):
        return pltpu.make_async_remote_copy(
            src_ref=src,
            dst_ref=src,
            send_sem=place_send.at[slot],
            recv_sem=place_recv.at[slot],
            device_id=peer,
            device_id_type=pl.DeviceIdType.MESH,
        )

    shared = []
    for base, src, targets in (
        (0, places.at[zh, y, x], peers[0:3]),
        (3, places.at[zh, y], peers[3:6]),
        (6, places.at[zh], peers[6:7]),
    ):
        stage = [share(src, base + k, peer) for k, peer in enumerate(targets)]
        for copy in stage:
            copy.start()
        for copy in stage:
            copy.wait_recv()
        shared += stage

    halves = []
    rest = list(rest)
    parts = []
    for c, (_, rows) in enumerate(CHUNKS):
        pair = []
        for h in range(2):
            part, o1, r1, l1, o2, r2, l2, zb = rest[:8]
            rest = rest[8:]
            first, second = (("x", x), ("y", y)) if h == 0 else (("y", y), ("x", x))
            pair.append(
                Half(
                    part,
                    ((o1, r1, l1), (o2, r2, l2)),
                    zb,
                    send.at[c, h],
                    recv.at[c, h],
                    rows,
                    first,
                    second,
                    zh,
                    dev,
                )
            )
        halves.append(pair)

    def multiply(t, carry):
        xd, yd, zd = place_of(t)
        dest = (zd * NY + yd) * NX + xd
        slot = lax.rem(t, SLOTS)
        load(t).wait()
        rows_iota = lax.broadcasted_iota(jnp.int32, (LR, LR), 0).astype(F32)
        pick = (rows_iota == places[zd, yd, xd]).astype(F32).astype(BF16)
        for b in range(probes.shape[0] // LR):
            cols = pl.ds(b * LR, LR)
            moved = jnp.dot(pick, slots[slot, :, cols], preferred_element_type=F32)
            own = leaf * (probes.shape[0] // LR) + b == grp * (NX * NY * NZ) + dest
            permuted[:, cols] = jnp.where(own, 0.0, moved).astype(BF16)
        for h in range(2):
            product = jnp.dot(
                permuted[...], probes[:, pl.ds(h * HALF, HALF)], preferred_element_type=F32
            )
            for c, (row, rows) in enumerate(CHUNKS):
                at = (xd, yd, zd) if h == 0 else (yd, xd, zd)
                halves[c][h].part[at] = product[row : row + rows]

        @pl.when(t + SLOTS < NX * NY * NZ)
        def _():
            load(t + SLOTS).start()

        return carry

    a, b = halves
    lax.fori_loop(0, 8, multiply, 0)
    a[0].start(0, OPP_R, OPP_L)
    lax.fori_loop(8, 14, multiply, 0)
    a[1].start(0, OPP_R, OPP_L)
    lax.fori_loop(14, 20, multiply, 0)
    a[0].start(0, NEAR_RB)
    lax.fori_loop(20, 26, multiply, 0)
    a[0].start(0, NEAR_LA)
    lax.fori_loop(26, 32, multiply, 0)
    a[1].start(0, NEAR_RB, NEAR_LA)
    for h in range(2):
        a[h].relay(0)
    for h in range(2):
        b[h].start(0, OPP_R, OPP_L)
    for h in range(2):
        a[h].gather(0)
        a[h].start(1, OPP_R, OPP_L, NEAR_RB, NEAR_LA)
    for h in range(2):
        b[h].start(0, NEAR_RB, NEAR_LA)
    for h in range(2):
        a[h].relay(1)
    for h in range(2):
        a[h].gather(1)
        a[h].z_start()
    for h in range(2):
        b[h].relay(0)

    def climb(src, c, slot, sem, to):
        return pltpu.make_async_remote_copy(
            src_ref=src.at[c],
            dst_ref=stack.at[c, slot],
            send_sem=tree_send.at[sem, c],
            recv_sem=tree_recv.at[slot, c],
            device_id=device_of(to),
            device_id_type=pl.DeviceIdType.MESH,
        )

    for h in range(2):
        rows = a[h].z_finish()
        for c in range(2 * h, 2 * h + 2):
            piece = rows[:, (c - 2 * h) * PIECE : (c - 2 * h + 1) * PIECE]
            leaf_rows[c] = piece

            @pl.when(odd)
            def _():
                stack[c, 1] = leaf_rows[c]

            @pl.when(jnp.logical_not(odd))
            def _():
                climb(leaf_rows, c, 0, 0, me + 1).start()

    sends = level < LEVELS
    below_root = level == LEVELS - 1
    for c in range(PIECES):
        climb(leaf_rows, c, 0, 0, me + 1).wait_recv()

        @pl.when(jnp.logical_not(odd))
        def _():
            climb(leaf_rows, c, 1, 0, me + 1).wait_recv()

        node_rows[c] = select(node_pick, stack[c].reshape(LR, PIECE))

        @pl.when(sends)
        def _():
            climb(node_rows, c, side, 1, parent).start()

        @pl.when(below_root)
        def _():
            climb(node_rows, c, side, 2, 0).start()

    grams = []
    for rows in (leaf_rows, node_rows):
        gram = 0.0
        for c in range(PIECES):
            gram = gram + times_transposed(rows[c], rows[c])
        grams.append(gram)
    leaf_inv, node_inv = inverses(grams)
    known = 0.0
    basis = 0.0
    for c in range(PIECES):
        weight = jnp.dot(leaf_inv, leaf_rows[c], precision=HIGHEST, preferred_element_type=F32)
        weights[c] = weight
        known = known + times_transposed(leaf_rows[c], weight)
        weight = jnp.dot(node_inv, node_rows[c], precision=HIGHEST, preferred_element_type=F32)
        basis = basis + times_transposed(stack[c].reshape(LR, PIECE), weight)
    node_out[0] = basis
    leaf_out[...] = select(unpick[:, :RANK].astype(BF16), known)

    for h in range(2):
        b[h].gather(0)
        b[h].start(1, OPP_R, OPP_L, NEAR_RB, NEAR_LA)
    for h in range(2):
        b[h].relay(1)
    for h in range(2):
        b[h].gather(1)
        b[h].z_start()
    basis = 0.0
    for h in range(2):
        rows = b[h].z_finish()
        for c in range(2):
            basis = basis + times_transposed(
                rows[:, c * PIECE : (c + 1) * PIECE], weights[2 * h + c]
            )
    leaf_out[...] += select(unpick[:, RANK:].astype(BF16), basis)

    for c in range(PIECES):

        @pl.when(jnp.logical_not(odd))
        def _():
            climb(leaf_rows, c, 0, 0, me + 1).wait_send()

        @pl.when(sends)
        def _():
            climb(node_rows, c, side, 1, parent).wait_send()

        @pl.when(below_root)
        def _():
            climb(node_rows, c, side, 2, 0).wait_send()

    for copy in shared:
        copy.wait_send()
    for pair in halves:
        for half in pair:
            for copy in half.started:
                copy.wait_send()


def bases(matrix, probes, skel, node_skel):
    depth = probes.shape[0]
    scratch = [
        pltpu.VMEM((SLOTS, LR, depth), BF16),
        pltpu.VMEM((LR, depth), BF16),
        pltpu.VMEM((NZ, NY, NX, 1, LR), F32),
        pltpu.VMEM((PIECES, RANK, PIECE), F32),
        pltpu.VMEM((PIECES, RANK, PIECE), F32),
        pltpu.VMEM((PIECES, 2, RANK, PIECE), F32),
        pltpu.VMEM((LR, LR), F32),
        pltpu.VMEM((PIECES, RANK, PIECE), F32),
        pltpu.SemaphoreType.DMA((SLOTS,)),
        pltpu.SemaphoreType.DMA((7,)),
        pltpu.SemaphoreType.DMA((7,)),
        pltpu.SemaphoreType.DMA((3, PIECES)),
        pltpu.SemaphoreType.DMA((2, PIECES)),
        pltpu.SemaphoreType.DMA((len(CHUNKS), 2, N_COPY)),
        pltpu.SemaphoreType.DMA((len(CHUNKS), 2, N_COPY)),
    ]
    for _, rows in CHUNKS:
        for _ in range(2):
            scratch += [
                pltpu.VMEM((4, 4, NZ, rows, HALF), F32),
                pltpu.VMEM((2, 4, NZ, rows // 2, HALF), F32),
                pltpu.VMEM((4, NZ, rows, HALF), F32),
                pltpu.VMEM((4, NZ, rows, HALF), F32),
                pltpu.VMEM((2, NZ, rows // 2, HALF), F32),
                pltpu.VMEM((NZ, rows, HALF), F32),
                pltpu.VMEM((NZ, rows, HALF), F32),
                pltpu.VMEM((rows, HALF), F32),
            ]
    vmem = pl.BlockSpec(memory_space=pltpu.VMEM)
    return pl.pallas_call(
        kernel,
        out_shape=(
            jax.ShapeDtypeStruct((LR, RANK), F32),
            jax.ShapeDtypeStruct((1, LR, RANK), F32),
        ),
        in_specs=[pl.BlockSpec(memory_space=pl.ANY), vmem, vmem, vmem],
        out_specs=(vmem, vmem),
        scratch_shapes=scratch,
        compiler_params=pltpu.CompilerParams(
            collective_id=0, has_side_effects=True, vmem_limit_bytes=56 * 2**20
        ),
        name="bases",
    )(matrix, probes, skel, node_skel)


def on_device(matrix, probes, leaf_skeleton, node_skeleton):
    return bases(matrix, probes, leaf_skeleton, node_skeleton)


def solution(mesh):
    return jax.shard_map(
        on_device,
        mesh=mesh,
        in_specs=(P("grp", "leaf"), P("leaf", None), P(("grp", "leaf"), None), P()),
        out_specs=(P(("grp", "leaf"), None), P(("grp", "leaf"), None, None)),
        check_vma=False,
    )
```

```python
import jax
import jax.numpy as jnp
from jax import lax
from jax.experimental import pallas as pl
from jax.experimental.pallas import tpu as pltpu
from jax.sharding import PartitionSpec as P

NX, NY, NZ = 4, 4, 2
LR = 256
RANK = 128
HALF = 256
SLOTS = 8
CHUNKS = ((0, 128, False), (128, 64, False), (192, 64, True))
PIECES = 4
PIECE = 128
LEVELS = 7
GROUP = NX * NY * NZ
LEAVES = 128
PANEL = 16
HIGHEST = lax.Precision.HIGHEST
F32 = jnp.float32
BF16 = jnp.bfloat16
ORDER = (
    [(2, 0), (2, 1), (2, 2), (2, 3)]
    + [(0, 2), (1, 2), (3, 2)]
    + [(1, 0), (1, 1), (1, 3)]
    + [(3, 0), (3, 1), (3, 3)]
    + [(0, 1), (0, 3), (0, 0)]
)
OPP_R, OPP_L, NEAR_RA, NEAR_RB, NEAR_LA, NEAR_LB = range(6)
PASS = 6
Z_COPY = 2 * PASS
N_COPY = 2 * PASS + 4


def mod4(v):
    return lax.rem(v + 4, 4)


class Half:
    def __init__(self, part, bufs, zbuf, send, recv, rows, z_first, first, second, zh, dev):
        self.whole, self.bufs, self.zbuf = part, bufs, zbuf
        self.part = part.at[zh] if z_first else part
        self.send, self.recv = send, recv
        self.rows = rows
        self.z_first = z_first
        self.axes = (first, second)
        self.zh = zh
        self.dev = dev
        self.started = []

    def block(self, phase, index):
        if phase == 0:
            return self.part.at[index]
        return self.part.at[self.axes[0][1], index]

    def lead(self, phase):
        return 2 - phase - self.z_first

    def begin(self, copy):
        copy.start()
        self.started.append(copy)

    def remote(self, src, dst, slot, to):
        return pltpu.make_async_remote_copy(
            src_ref=src,
            dst_ref=dst,
            send_sem=self.send.at[slot],
            recv_sem=self.recv.at[slot],
            device_id=to,
            device_id_type=pl.DeviceIdType.MESH,
        )

    def copy(self, phase, kind):
        name, me = self.axes[phase]
        half = self.rows // 2
        opp, near_r, near_l = self.bufs[phase]
        lo, hi = pl.ds(0, half), pl.ds(half, half)
        lead = (slice(None),) * self.lead(phase)
        right, left = mod4(me + 1), mod4(me - 1)
        index, rows, dst, to = {
            OPP_R: (mod4(me + 2), lo, opp.at[0], right),
            OPP_L: (mod4(me + 2), hi, opp.at[1], left),
            NEAR_RA: (right, lo, near_r.at[(*lead, lo)], right),
            NEAR_RB: (right, hi, near_r.at[(*lead, hi)], right),
            NEAR_LA: (left, lo, near_l.at[(*lead, lo)], left),
            NEAR_LB: (left, hi, near_l.at[(*lead, hi)], left),
        }[kind]
        return self.remote(
            self.block(phase, index).at[(*lead, rows)],
            dst,
            phase * PASS + kind,
            self.dev(**{name: to}),
        )

    def start(self, phase, *kinds):
        for kind in kinds:
            self.begin(self.copy(phase, kind))

    def wait(self, phase, kind):
        self.copy(phase, kind).wait_recv()

    def relay(self, phase):
        me = self.axes[phase][1]
        half = self.rows // 2
        opp = self.bufs[phase][0]
        for kind, side, index, row, on in (
            (OPP_R, 0, mod4(me + 1), 0, NEAR_RA),
            (OPP_L, 1, mod4(me - 1), half, NEAR_LB),
        ):
            self.wait(phase, kind)
            self.add(self.block(phase, index), phase, row, half, (opp.at[side],))
            self.start(phase, on)

    def gather(self, phase):
        me = self.axes[phase][1]
        for kind in (NEAR_RB, NEAR_LA, NEAR_RA, NEAR_LB):
            self.wait(phase, kind)
        self.add(self.block(phase, me), phase, 0, self.rows, self.bufs[phase][1:])

    def add(self, target, phase, row, count, terms):
        rows, term_rows = pl.ds(row, count), pl.ds(0, count)

        def step(at):
            value = target[(*at, rows)]
            for term in terms:
                value = value + term[(*at, term_rows)]
            target[(*at, rows)] = value

        if self.lead(phase) == 0:
            step(())
        elif self.lead(phase) == 1:
            lax.fori_loop(0, NZ if phase else 4, lambda i, c: (step((i,)), c)[1], 0)
        else:
            lax.fori_loop(0, 4 * NZ, lambda i, c: (step((i // NZ, lax.rem(i, NZ))), c)[1], 0)

    def z_copy(self, x=None):
        to = self.dev(z=1 - self.zh)
        if not self.z_first:
            src = self.part.at[self.axes[0][1], self.axes[1][1], 1 - self.zh]
            return self.remote(src, self.zbuf, 2 * PASS, to)
        steps, x = x
        at = (x,) if self.axes[0][0] == "x" else (slice(None), x)
        return self.remote(
            self.whole.at[(1 - self.zh, *at)], self.zbuf.at[at], 2 * PASS + steps, to
        )

    def z_start(self, x=None):
        self.begin(self.z_copy(x))

    def z_merge(self, xs):
        for x in xs:
            self.z_copy(x).wait_recv()

        def step(i, carry):
            at = (i // 4, lax.rem(i, 4))
            self.part[at] += self.zbuf[at]
            return carry

        lax.fori_loop(0, 16, step, 0)

    def finish(self):
        at = (self.axes[0][1], self.axes[1][1])
        if self.z_first:
            return self.part[at]
        self.z_copy().wait_recv()
        return self.part[(*at, self.zh)] + self.zbuf[...]


def leaf_order(skel):
    hit = (lax.broadcasted_iota(jnp.int32, (LR, RANK), 0) == skel).astype(F32).astype(BF16)
    picked = lax.dot_general(
        jnp.ones((8, RANK), BF16), hit, (((1,), (1,)), ((), ())), preferred_element_type=F32
    )
    before = (
        (
            lax.broadcasted_iota(jnp.int32, (LR, LR), 0)
            < lax.broadcasted_iota(jnp.int32, (LR, LR), 1)
        )
        .astype(F32)
        .astype(BF16)
    )
    count = jnp.dot(picked.astype(BF16), before, preferred_element_type=F32)
    lane = lax.broadcasted_iota(jnp.int32, (8, LR), 1).astype(F32)
    place = jnp.where(picked > 0.5, count, RANK + lane - count)
    return place[0:1]


def selection(place):
    return (lax.broadcasted_iota(jnp.int32, (LR, LR), 0).astype(F32) == place).astype(F32)


def select(pick, value):
    total = 0.0
    for _ in range(3):
        term = value.astype(BF16)
        total = total + jnp.dot(pick, term, preferred_element_type=F32)
        value = value - term.astype(F32)
    return total


def times_transposed(a, b):
    return lax.dot_general(
        a, b, (((1,), (1,)), ((), ())), precision=HIGHEST, preferred_element_type=F32
    )


def eliminate(panels):
    lane = lax.broadcasted_iota(jnp.int32, panels[0].shape, 1)
    sub = lax.broadcasted_iota(jnp.int32, panels[0].shape, 0)
    for k in range(PANEL):
        done = []
        for p in panels:
            row = jnp.where(lane[0:1] == k, 1.0, p[k : k + 1]) * (1.0 / p[k : k + 1, k : k + 1])
            rest = jnp.where(lane == k, 0.0, p) - p[:, k : k + 1] * row
            done.append(jnp.where(sub == k, row, rest))
        panels = done
    return panels


def inverses(grams):
    def body(_, grams):
        panels = eliminate([g[:PANEL] for g in grams])
        done = []
        for g, p in zip(grams, panels):
            rest = g[PANEL:]
            lane = lax.broadcasted_iota(jnp.int32, rest.shape, 1)
            rest = jnp.where(lane < PANEL, 0.0, rest) - jnp.dot(
                rest[:, :PANEL], p, precision=HIGHEST, preferred_element_type=F32
            )
            done.append(pltpu.roll(jnp.concatenate([rest, p], 0), RANK - PANEL, 1))
        return tuple(done)

    return lax.fori_loop(0, RANK // PANEL, body, tuple(grams))


def kernel(
    matrix,
    probes,
    skel,
    node_skel,
    leaf_out,
    node_out,
    slots,
    permuted,
    places,
    leaf_rows,
    node_rows,
    stack,
    unpick,
    weights,
    in_sem,
    place_send,
    place_recv,
    tree_send,
    tree_recv,
    send,
    recv,
    *rest,
):
    leaf = lax.axis_index("leaf")
    grp = lax.axis_index("grp")
    x = lax.rem(leaf, NX)
    y = lax.rem(leaf // NX, NY)
    zh = leaf // (NX * NY)

    def dev(x=x, y=y, z=zh):
        return {"leaf": (z * NY + y) * NX + x}

    barrier = pltpu.get_barrier_semaphore()

    def peer(k):
        return {"leaf": lax.rem(leaf + k, GROUP)}

    def greet_peer(k, carry):
        pl.semaphore_signal(barrier, 1, device_id=peer(k), device_id_type=pl.DeviceIdType.MESH)
        return carry

    lax.fori_loop(1, GROUP, greet_peer, 0)

    me = grp * GROUP + leaf
    odd = lax.rem(me, 2) == 1
    level = jnp.int32(1)
    for k in range(1, LEVELS):
        level = jnp.where(lax.rem(me, 2**k) == 0, k + 1, level)
    step = sum(jnp.where(level == k, 2 ** (k - 1), 0) for k in range(1, LEVELS + 1))
    node = sum(
        jnp.where(level == k, LEAVES - (LEAVES >> (k - 1)) + me // 2**k, 0)
        for k in range(1, LEVELS + 1)
    )
    side = lax.rem(me // (2 * step), 2)
    parent = jnp.where(side == 0, me + step, me - step)
    top = me == 0

    def device_of(number):
        number = lax.rem(number + LEAVES, LEAVES)
        return {"grp": number // GROUP, "leaf": lax.rem(number, GROUP)}

    def greet(number):
        pl.semaphore_signal(
            barrier, 1, device_id=device_of(number), device_id_type=pl.DeviceIdType.MESH
        )

    @pl.when(odd)
    def _():
        greet(me - 1)

    @pl.when(jnp.logical_not(odd))
    def _():
        greet(jnp.where(top, LEAVES // 4, me - step // 2))
        greet(jnp.where(top, 3 * LEAVES // 4, me + step // 2))

    greeted = GROUP - 1 + jnp.where(odd, 0, 1)
    greeted = greeted + jnp.where(level < LEVELS, 1, 0) + jnp.where(level == LEVELS - 1, 1, 0)

    def place_of(t):
        pair = t // NZ
        i = sum(jnp.where(pair == k, o[0], 0) for k, o in enumerate(ORDER))
        j = sum(jnp.where(pair == k, o[1], 0) for k, o in enumerate(ORDER))
        return mod4(x + i), mod4(y + j), lax.rem(t, NZ)

    def load(t):
        xd, yd, zd = place_of(t)
        dest = (zd * NY + yd) * NX + xd
        slot = lax.rem(t, SLOTS)
        return pltpu.make_async_copy(
            matrix.at[pl.ds(pl.multiple_of(dest * LR, LR), LR), :],
            slots.at[slot],
            in_sem.at[slot],
        )

    def prefetch(t, carry):
        load(t).start()
        return carry

    lax.fori_loop(0, SLOTS, prefetch, 0)

    place = leaf_order(skel[...])
    places[leaf] = place
    pl.semaphore_wait(barrier, greeted)

    def share(k):
        return pltpu.make_async_remote_copy(
            src_ref=places.at[leaf],
            dst_ref=places.at[leaf],
            send_sem=place_send.at[k - 1],
            recv_sem=place_recv.at[k - 1],
            device_id=peer(k),
            device_id_type=pl.DeviceIdType.MESH,
        )

    def share_start(k, carry):
        share(k).start()
        return carry

    def share_arrived(k, carry):
        share(k).wait_recv()
        return carry

    def share_sent(k, carry):
        share(k).wait_send()
        return carry

    lax.fori_loop(1, GROUP, share_start, 0)
    node_pick = selection(leaf_order(node_skel[pl.ds(node, 1), :]))[:RANK].astype(BF16)
    unpick[...] = selection(place).T
    lax.fori_loop(1, GROUP, share_arrived, 0)

    halves = []
    rest = list(rest)
    parts = []
    for c, (_, rows, z_first) in enumerate(CHUNKS):
        pair = []
        for h in range(2):
            part, o1, r1, l1, o2, r2, l2, zb = rest[:8]
            rest = rest[8:]
            first, second = (("x", x), ("y", y)) if h == 0 else (("y", y), ("x", x))
            pair.append(
                Half(
                    part,
                    ((o1, r1, l1), (o2, r2, l2)),
                    zb,
                    send.at[c, h],
                    recv.at[c, h],
                    rows,
                    z_first,
                    first,
                    second,
                    zh,
                    dev,
                )
            )
        halves.append(pair)

    def multiply(t, carry):
        xd, yd, zd = place_of(t)
        dest = (zd * NY + yd) * NX + xd
        slot = lax.rem(t, SLOTS)
        load(t).wait()
        rows_iota = lax.broadcasted_iota(jnp.int32, (LR, LR), 0).astype(F32)
        pick = (rows_iota == places[dest]).astype(F32).astype(BF16)
        for b in range(probes.shape[0] // LR):
            cols = pl.ds(b * LR, LR)
            moved = jnp.dot(pick, slots[slot, :, cols], preferred_element_type=F32)
            own = leaf * (probes.shape[0] // LR) + b == grp * (NX * NY * NZ) + dest
            permuted[:, cols] = jnp.where(own, 0.0, moved).astype(BF16)
        for h in range(2):
            product = jnp.dot(
                permuted[...], probes[:, pl.ds(h * HALF, HALF)], preferred_element_type=F32
            )
            for c, (row, rows, z_first) in enumerate(CHUNKS):
                at = (xd, yd) if h == 0 else (yd, xd)
                at = (zd, *at) if z_first else (*at, zd)
                halves[c][h].whole[at] = product[row : row + rows]

        @pl.when(t + SLOTS < NX * NY * NZ)
        def _():
            load(t + SLOTS).start()

        return carry

    a, b, d = halves
    xs = [(k, mod4(x + k)) for k in range(4)]
    lax.fori_loop(0, 8, multiply, 0)
    a[0].start(0, OPP_R, OPP_L)
    for h in range(2):
        d[h].z_start(xs[2])
    lax.fori_loop(8, 14, multiply, 0)
    a[1].start(0, OPP_R, OPP_L)
    lax.fori_loop(14, 20, multiply, 0)
    a[0].start(0, NEAR_RB)
    for h in range(2):
        d[h].z_start(xs[1])
    lax.fori_loop(20, 26, multiply, 0)
    a[0].start(0, NEAR_LA)
    for h in range(2):
        d[h].z_start(xs[3])
    lax.fori_loop(26, 32, multiply, 0)
    a[1].start(0, NEAR_RB, NEAR_LA)
    for h in range(2):
        d[h].z_start(xs[0])
    for h in range(2):
        a[h].relay(0)
    for h in range(2):
        a[h].gather(0)
        a[h].start(1, OPP_R, OPP_L, NEAR_RB, NEAR_LA)
    for h in range(2):
        b[h].start(0, OPP_R, OPP_L)
    for h in range(2):
        a[h].relay(1)
    for h in range(2):
        b[h].start(0, NEAR_RB, NEAR_LA)
    for h in range(2):
        a[h].gather(1)
        a[h].z_start()
    for h in range(2):
        b[h].relay(0)

    def climb(src, c, slot, sem, to):
        return pltpu.make_async_remote_copy(
            src_ref=src.at[c],
            dst_ref=stack.at[c, slot],
            send_sem=tree_send.at[sem, c],
            recv_sem=tree_recv.at[slot, c],
            device_id=device_of(to),
            device_id_type=pl.DeviceIdType.MESH,
        )

    for h in range(2):
        rows = a[h].finish()
        for c in range(2 * h, 2 * h + 2):
            piece = rows[:, (c - 2 * h) * PIECE : (c - 2 * h + 1) * PIECE]
            leaf_rows[c] = piece

            @pl.when(odd)
            def _():
                stack[c, 1] = leaf_rows[c]

            @pl.when(jnp.logical_not(odd))
            def _():
                climb(leaf_rows, c, 0, 0, me + 1).start()

    sends = level < LEVELS
    below_root = level == LEVELS - 1

    def tree(low, high):
        @pl.when(jnp.logical_and(level >= low, level <= high))
        def _():
            for c in range(PIECES):
                climb(leaf_rows, c, 0, 0, me + 1).wait_recv()

                @pl.when(jnp.logical_not(odd))
                def _():
                    climb(leaf_rows, c, 1, 0, me + 1).wait_recv()

                node_rows[c] = select(node_pick, stack[c].reshape(LR, PIECE))

                @pl.when(sends)
                def _():
                    climb(node_rows, c, side, 1, parent).start()

                @pl.when(below_root)
                def _():
                    climb(node_rows, c, side, 2, 0).start()

    def gram_of(rows):
        gram = 0.0
        for c in range(PIECES):
            gram = gram + times_transposed(rows[c], rows[c])
        return gram

    tree(1, 2)
    for h in range(2):
        b[h].gather(0)
        b[h].start(1, OPP_R, OPP_L, NEAR_RB, NEAR_LA)
    tree(3, 3)
    for h in range(2):
        b[h].relay(1)
    tree(4, 4)
    for h in range(2):
        d[h].z_merge(xs)
        d[h].start(0, OPP_R, OPP_L, NEAR_RB, NEAR_LA)
    tree(5, 5)
    for h in range(2):
        b[h].gather(1)
        b[h].z_start()
    for h in range(2):
        d[h].relay(0)
    tree(6, 6)
    for h in range(2):
        d[h].gather(0)
        d[h].start(1, OPP_R, OPP_L, NEAR_RB, NEAR_LA)
    tree(7, 7)
    for h in range(2):
        d[h].relay(1)
    leaf_inv, node_inv = inverses((gram_of(leaf_rows), gram_of(node_rows)))
    known = 0.0
    basis = 0.0
    for c in range(PIECES):
        weight = jnp.dot(leaf_inv, leaf_rows[c], precision=HIGHEST, preferred_element_type=F32)
        weights[c] = weight
        known = known + times_transposed(leaf_rows[c], weight)
        weight = jnp.dot(node_inv, node_rows[c], precision=HIGHEST, preferred_element_type=F32)
        basis = basis + times_transposed(stack[c].reshape(LR, PIECE), weight)
    node_out[0] = basis
    leaf_out[...] = select(unpick[:, :RANK].astype(BF16), known)

    found = []
    for part in (b, d):
        basis = 0.0
        for h in range(2):
            if part is d:
                part[h].gather(1)
            rows = part[h].finish()
            for c in range(2):
                basis = basis + times_transposed(
                    rows[:, c * PIECE : (c + 1) * PIECE], weights[2 * h + c]
                )
        found.append(basis)
    leaf_out[...] += select(unpick[:, RANK:].astype(BF16), jnp.concatenate(found, 0))

    for c in range(PIECES):

        @pl.when(jnp.logical_not(odd))
        def _():
            climb(leaf_rows, c, 0, 0, me + 1).wait_send()

        @pl.when(sends)
        def _():
            climb(node_rows, c, side, 1, parent).wait_send()

        @pl.when(below_root)
        def _():
            climb(node_rows, c, side, 2, 0).wait_send()

    lax.fori_loop(1, GROUP, share_sent, 0)
    for pair in halves:
        for half in pair:
            for copy in half.started:
                copy.wait_send()


def bases(matrix, probes, skel, node_skel):
    depth = probes.shape[0]
    scratch = [
        pltpu.VMEM((SLOTS, LR, depth), BF16),
        pltpu.VMEM((LR, depth), BF16),
        pltpu.VMEM((GROUP, 1, LR), F32),
        pltpu.VMEM((PIECES, RANK, PIECE), F32),
        pltpu.VMEM((PIECES, RANK, PIECE), F32),
        pltpu.VMEM((PIECES, 2, RANK, PIECE), F32),
        pltpu.VMEM((LR, LR), F32),
        pltpu.VMEM((PIECES, RANK, PIECE), F32),
        pltpu.SemaphoreType.DMA((SLOTS,)),
        pltpu.SemaphoreType.DMA((GROUP - 1,)),
        pltpu.SemaphoreType.DMA((GROUP - 1,)),
        pltpu.SemaphoreType.DMA((3, PIECES)),
        pltpu.SemaphoreType.DMA((2, PIECES)),
        pltpu.SemaphoreType.DMA((len(CHUNKS), 2, N_COPY)),
        pltpu.SemaphoreType.DMA((len(CHUNKS), 2, N_COPY)),
    ]
    for _, rows, z_first in CHUNKS:
        z = () if z_first else (NZ,)
        for _ in range(2):
            scratch += [
                pltpu.VMEM((NZ, 4, 4, rows, HALF) if z_first else (4, 4, NZ, rows, HALF), F32),
                pltpu.VMEM((2, 4, *z, rows // 2, HALF), F32),
                pltpu.VMEM((4, *z, rows, HALF), F32),
                pltpu.VMEM((4, *z, rows, HALF), F32),
                pltpu.VMEM((2, *z, rows // 2, HALF), F32),
                pltpu.VMEM((*z, rows, HALF), F32),
                pltpu.VMEM((*z, rows, HALF), F32),
                pltpu.VMEM((4, 4, rows, HALF) if z_first else (rows, HALF), F32),
            ]
    vmem = pl.BlockSpec(memory_space=pltpu.VMEM)
    return pl.pallas_call(
        kernel,
        out_shape=(
            jax.ShapeDtypeStruct((LR, RANK), F32),
            jax.ShapeDtypeStruct((1, LR, RANK), F32),
        ),
        in_specs=[pl.BlockSpec(memory_space=pl.ANY), vmem, vmem, vmem],
        out_specs=(vmem, vmem),
        scratch_shapes=scratch,
        compiler_params=pltpu.CompilerParams(
            collective_id=0, has_side_effects=True, vmem_limit_bytes=56 * 2**20
        ),
        name="bases",
    )(matrix, probes, skel, node_skel)


def on_device(matrix, probes, leaf_skeleton, node_skeleton):
    return bases(matrix, probes, leaf_skeleton, node_skeleton)


def solution(mesh):
    return jax.shard_map(
        on_device,
        mesh=mesh,
        in_specs=(P("grp", "leaf"), P("leaf", None), P(("grp", "leaf"), None), P()),
        out_specs=(P(("grp", "leaf"), None), P(("grp", "leaf"), None, None)),
        check_vma=False,
    )
```

```python
import jax
import jax.numpy as jnp
from jax import lax
from jax.experimental import pallas as pl
from jax.experimental.pallas import tpu as pltpu
from jax.sharding import PartitionSpec as P

NX, NY, NZ = 4, 4, 2
LR = 256
RANK = 128
HALF = 256
SLOTS = 8
CHUNKS = ((0, 64, False), (64, 64, False), (128, 64, False), (192, 64, True))
PIECES = 4
PIECE = 128
LEVELS = 7
GROUP = NX * NY * NZ
LEAVES = 128
PANEL = 16
AHEAD = 8
HIGHEST = lax.Precision.HIGHEST
F32 = jnp.float32
BF16 = jnp.bfloat16
ORDER = (
    [(2, 0), (2, 1), (2, 2), (2, 3)]
    + [(0, 2), (1, 2), (3, 2)]
    + [(1, 0), (1, 1), (1, 3)]
    + [(3, 0), (3, 1), (3, 3)]
    + [(0, 1), (0, 3), (0, 0)]
)
OPP_R, OPP_L, NEAR_RA, NEAR_RB, NEAR_LA, NEAR_LB = range(6)
PASS = 6
Z_COPY = 2 * PASS
N_COPY = 2 * PASS + 4


def mod4(v):
    return lax.rem(v + 4, 4)


class Half:
    def __init__(self, part, bufs, zbuf, send, recv, rows, z_first, first, second, zh, dev):
        self.whole, self.bufs, self.zbuf = part, bufs, zbuf
        self.part = part.at[zh] if z_first else part
        self.send, self.recv = send, recv
        self.rows = rows
        self.z_first = z_first
        self.axes = (first, second)
        self.zh = zh
        self.dev = dev
        self.started = []

    def block(self, phase, index):
        if phase == 0:
            return self.part.at[index]
        return self.part.at[self.axes[0][1], index]

    def lead(self, phase):
        return 2 - phase - self.z_first

    def begin(self, copy):
        copy.start()
        self.started.append(copy)

    def remote(self, src, dst, slot, to):
        return pltpu.make_async_remote_copy(
            src_ref=src,
            dst_ref=dst,
            send_sem=self.send.at[slot],
            recv_sem=self.recv.at[slot],
            device_id=to,
            device_id_type=pl.DeviceIdType.MESH,
        )

    def copy(self, phase, kind):
        name, me = self.axes[phase]
        half = self.rows // 2
        opp, near_r, near_l = self.bufs[phase]
        lo, hi = pl.ds(0, half), pl.ds(half, half)
        lead = (slice(None),) * self.lead(phase)
        right, left = mod4(me + 1), mod4(me - 1)
        index, rows, dst, to = {
            OPP_R: (mod4(me + 2), lo, opp.at[0], right),
            OPP_L: (mod4(me + 2), hi, opp.at[1], left),
            NEAR_RA: (right, lo, near_r.at[(*lead, lo)], right),
            NEAR_RB: (right, hi, near_r.at[(*lead, hi)], right),
            NEAR_LA: (left, lo, near_l.at[(*lead, lo)], left),
            NEAR_LB: (left, hi, near_l.at[(*lead, hi)], left),
        }[kind]
        return self.remote(
            self.block(phase, index).at[(*lead, rows)],
            dst,
            phase * PASS + kind,
            self.dev(**{name: to}),
        )

    def start(self, phase, *kinds):
        for kind in kinds:
            self.begin(self.copy(phase, kind))

    def wait(self, phase, kind):
        self.copy(phase, kind).wait_recv()

    def relay(self, phase):
        me = self.axes[phase][1]
        half = self.rows // 2
        opp = self.bufs[phase][0]
        for kind, side, index, row, on in (
            (OPP_R, 0, mod4(me + 1), 0, NEAR_RA),
            (OPP_L, 1, mod4(me - 1), half, NEAR_LB),
        ):
            self.wait(phase, kind)
            self.add(self.block(phase, index), phase, row, half, (opp.at[side],))
            self.start(phase, on)

    def gather(self, phase):
        me = self.axes[phase][1]
        for kind in (NEAR_RB, NEAR_LA, NEAR_RA, NEAR_LB):
            self.wait(phase, kind)
        self.add(self.block(phase, me), phase, 0, self.rows, self.bufs[phase][1:])

    def add(self, target, phase, row, count, terms):
        rows, term_rows = pl.ds(row, count), pl.ds(0, count)

        def step(at):
            value = target[(*at, rows)]
            for term in terms:
                value = value + term[(*at, term_rows)]
            target[(*at, rows)] = value

        if self.lead(phase) == 0:
            step(())
        elif self.lead(phase) == 1:
            lax.fori_loop(0, NZ if phase else 4, lambda i, c: (step((i,)), c)[1], 0)
        else:
            lax.fori_loop(0, 4 * NZ, lambda i, c: (step((i // NZ, lax.rem(i, NZ))), c)[1], 0)

    def z_copy(self, x=None):
        to = self.dev(z=1 - self.zh)
        if not self.z_first:
            src = self.part.at[self.axes[0][1], self.axes[1][1], 1 - self.zh]
            return self.remote(src, self.zbuf, 2 * PASS, to)
        steps, x = x
        at = (x,) if self.axes[0][0] == "x" else (slice(None), x)
        return self.remote(
            self.whole.at[(1 - self.zh, *at)], self.zbuf.at[at], 2 * PASS + steps, to
        )

    def z_start(self, x=None):
        self.begin(self.z_copy(x))

    def z_merge(self, xs):
        for x in xs:
            self.z_copy(x).wait_recv()

        def step(i, carry):
            at = (i // 4, lax.rem(i, 4))
            self.part[at] += self.zbuf[at]
            return carry

        lax.fori_loop(0, 16, step, 0)

    def finish(self):
        at = (self.axes[0][1], self.axes[1][1])
        if self.z_first:
            return self.part[at]
        self.z_copy().wait_recv()
        return self.part[(*at, self.zh)] + self.zbuf[...]


def leaf_order(skel):
    hit = (lax.broadcasted_iota(jnp.int32, (LR, RANK), 0) == skel).astype(F32).astype(BF16)
    picked = lax.dot_general(
        jnp.ones((8, RANK), BF16), hit, (((1,), (1,)), ((), ())), preferred_element_type=F32
    )
    before = (
        (
            lax.broadcasted_iota(jnp.int32, (LR, LR), 0)
            < lax.broadcasted_iota(jnp.int32, (LR, LR), 1)
        )
        .astype(F32)
        .astype(BF16)
    )
    count = jnp.dot(picked.astype(BF16), before, preferred_element_type=F32)
    lane = lax.broadcasted_iota(jnp.int32, (8, LR), 1).astype(F32)
    place = jnp.where(picked > 0.5, count, RANK + lane - count)
    return place[0:1]


def selection(place):
    return (lax.broadcasted_iota(jnp.int32, (LR, LR), 0).astype(F32) == place).astype(F32)


def select(pick, value):
    total = 0.0
    for _ in range(3):
        term = value.astype(BF16)
        total = total + jnp.dot(pick, term, preferred_element_type=F32)
        value = value - term.astype(F32)
    return total


def times_transposed(a, b):
    return lax.dot_general(
        a, b, (((1,), (1,)), ((), ())), precision=HIGHEST, preferred_element_type=F32
    )


def eliminate(panels):
    panels = list(panels)
    lane = lax.broadcasted_iota(jnp.int32, panels[0].shape, 1)
    sub = lax.broadcasted_iota(jnp.int32, panels[0].shape, 0)
    for base in range(0, PANEL, AHEAD):
        columns = [
            [jnp.broadcast_to(p[:, k : k + 1], p.shape) for k in range(base, base + AHEAD)]
            for p in panels
        ]
        for ahead in range(AHEAD):
            k = base + ahead
            for n, p in enumerate(panels):
                column = columns[n][ahead]
                scale = 1.0 / column[k : k + 1]
                row = jnp.where(lane[0:1] == k, 1.0, p[k : k + 1]) * scale
                rest = jnp.where(lane == k, 0.0, p) - column * row
                panels[n] = jnp.where(sub == k, row, rest)
                for later in range(ahead + 1, AHEAD):
                    other = columns[n][later]
                    row = other[k : k + 1] * scale
                    columns[n][later] = jnp.where(sub == k, row, other - column * row)
    return panels


def inverses(grams):
    def body(_, grams):
        panels = eliminate([g[:PANEL] for g in grams])
        done = []
        for g, p in zip(grams, panels):
            rest = g[PANEL:]
            lane = lax.broadcasted_iota(jnp.int32, rest.shape, 1)
            rest = jnp.where(lane < PANEL, 0.0, rest) - jnp.dot(
                rest[:, :PANEL], p, precision=HIGHEST, preferred_element_type=F32
            )
            done.append(pltpu.roll(jnp.concatenate([rest, p], 0), RANK - PANEL, 1))
        return tuple(done)

    return lax.fori_loop(0, RANK // PANEL, body, tuple(grams))


def kernel(
    matrix,
    probes,
    skel,
    node_skel,
    leaf_out,
    node_out,
    slots,
    permuted,
    places,
    leaf_rows,
    node_rows,
    stack,
    unpick,
    weights,
    in_sem,
    place_send,
    place_recv,
    tree_send,
    tree_recv,
    send,
    recv,
    *rest,
):
    leaf = lax.axis_index("leaf")
    grp = lax.axis_index("grp")
    x = lax.rem(leaf, NX)
    y = lax.rem(leaf // NX, NY)
    zh = leaf // (NX * NY)

    def dev(x=x, y=y, z=zh):
        return {"leaf": (z * NY + y) * NX + x}

    barrier = pltpu.get_barrier_semaphore()

    def peer(k):
        return {"leaf": lax.rem(leaf + k, GROUP)}

    def greet_peer(k, carry):
        pl.semaphore_signal(barrier, 1, device_id=peer(k), device_id_type=pl.DeviceIdType.MESH)
        return carry

    lax.fori_loop(1, GROUP, greet_peer, 0)

    me = grp * GROUP + leaf
    odd = lax.rem(me, 2) == 1
    level = jnp.int32(1)
    for k in range(1, LEVELS):
        level = jnp.where(lax.rem(me, 2**k) == 0, k + 1, level)
    step = sum(jnp.where(level == k, 2 ** (k - 1), 0) for k in range(1, LEVELS + 1))
    node = sum(
        jnp.where(level == k, LEAVES - (LEAVES >> (k - 1)) + me // 2**k, 0)
        for k in range(1, LEVELS + 1)
    )
    side = lax.rem(me // (2 * step), 2)
    parent = jnp.where(side == 0, me + step, me - step)
    top = me == 0

    def device_of(number):
        number = lax.rem(number + LEAVES, LEAVES)
        return {"grp": number // GROUP, "leaf": lax.rem(number, GROUP)}

    def greet(number):
        pl.semaphore_signal(
            barrier, 1, device_id=device_of(number), device_id_type=pl.DeviceIdType.MESH
        )

    @pl.when(odd)
    def _():
        greet(me - 1)

    @pl.when(jnp.logical_not(odd))
    def _():
        greet(jnp.where(top, LEAVES // 4, me - step // 2))
        greet(jnp.where(top, 3 * LEAVES // 4, me + step // 2))

    greeted = GROUP - 1 + jnp.where(odd, 0, 1)
    greeted = greeted + jnp.where(level < LEVELS, 1, 0) + jnp.where(level == LEVELS - 1, 1, 0)

    def steps_of(pair):
        i = sum(jnp.where(pair == k, o[0], 0) for k, o in enumerate(ORDER))
        j = sum(jnp.where(pair == k, o[1], 0) for k, o in enumerate(ORDER))
        return i, j

    def place_of(t):
        i, j = steps_of(t // NZ)
        return mod4(x + i), mod4(y + j), lax.rem(t, NZ)

    def load(t):
        xd, yd, zd = place_of(t)
        dest = (zd * NY + yd) * NX + xd
        slot = lax.rem(t, SLOTS)
        return pltpu.make_async_copy(
            matrix.at[pl.ds(pl.multiple_of(dest * LR, LR), LR), :],
            slots.at[slot],
            in_sem.at[slot],
        )

    def prefetch(t, carry):
        load(t).start()
        return carry

    lax.fori_loop(0, SLOTS, prefetch, 0)

    place = leaf_order(skel[...])
    places[leaf] = place
    pl.semaphore_wait(barrier, greeted)

    def share(pair, z):
        i, j = steps_of(pair)
        to = (z * NY + mod4(y - j)) * NX + mod4(x - i)
        copy = pltpu.make_async_remote_copy(
            src_ref=places.at[leaf],
            dst_ref=places.at[leaf],
            send_sem=place_send.at[NZ * pair + z],
            recv_sem=place_recv.at[NZ * pair + zh],
            device_id={"leaf": to},
            device_id_type=pl.DeviceIdType.MESH,
        )
        return to, copy

    def share_start(pair, carry):
        for z in range(NZ):
            to, copy = share(pair, z)
            pl.when(to != leaf)(copy.start)
        return carry

    def share_sent(pair, carry):
        for z in range(NZ):
            to, copy = share(pair, z)
            pl.when(to != leaf)(copy.wait_send)
        return carry

    def share_arrived(pair, z, dest):
        copy = pltpu.make_async_remote_copy(
            src_ref=places.at[dest],
            dst_ref=places.at[dest],
            send_sem=place_send.at[NZ * pair + z],
            recv_sem=place_recv.at[NZ * pair + z],
            device_id={"leaf": dest},
            device_id_type=pl.DeviceIdType.MESH,
        )
        pl.when(dest != leaf)(copy.wait_recv)

    lax.fori_loop(0, len(ORDER), share_start, 0)
    node_pick = selection(leaf_order(node_skel[pl.ds(node, 1), :]))[:RANK].astype(BF16)
    unpick[...] = selection(place).T

    halves = []
    rest = list(rest)
    parts = []
    for c, (_, rows, z_first) in enumerate(CHUNKS):
        pair = []
        for h in range(2):
            part, o1, r1, l1, o2, r2, l2, zb = rest[:8]
            rest = rest[8:]
            first, second = (("x", x), ("y", y)) if h == 0 else (("y", y), ("x", x))
            pair.append(
                Half(
                    part,
                    ((o1, r1, l1), (o2, r2, l2)),
                    zb,
                    send.at[c, h],
                    recv.at[c, h],
                    rows,
                    z_first,
                    first,
                    second,
                    zh,
                    dev,
                )
            )
        halves.append(pair)

    def multiply(pair, carry):
        i, j = steps_of(pair)
        xd, yd = mod4(x + i), mod4(y + j)
        rows_iota = lax.broadcasted_iota(jnp.int32, (LR, LR), 0).astype(F32)
        for zd in range(NZ):
            t = NZ * pair + zd
            dest = (zd * NY + yd) * NX + xd
            slot = lax.rem(t, SLOTS)
            load(t).wait()
            share_arrived(pair, zd, dest)
            pick = (rows_iota == places[dest]).astype(F32).astype(BF16)
            for block in range(probes.shape[0] // LR):
                cols = pl.ds(block * LR, LR)
                moved = jnp.dot(pick, slots[slot, :, cols], preferred_element_type=F32)
                own = leaf * (probes.shape[0] // LR) + block == grp * GROUP + dest
                permuted[zd, :, cols] = jnp.where(own, 0.0, moved).astype(BF16)
        for h in range(2):
            for zd in range(NZ):
                product = jnp.dot(
                    permuted[zd], probes[:, pl.ds(h * HALF, HALF)], preferred_element_type=F32
                )
                for c, (row, rows, z_first) in enumerate(CHUNKS):
                    at = (xd, yd) if h == 0 else (yd, xd)
                    at = (zd, *at) if z_first else (*at, zd)
                    halves[c][h].whole[at] = product[row : row + rows]

        @pl.when(NZ * pair + SLOTS < GROUP)
        def _():
            for zd in range(NZ):
                load(NZ * pair + zd + SLOTS).start()

        return carry

    a, e, b, d = halves
    xs = [(k, mod4(x + k)) for k in range(4)]

    def z_parts(k):
        for h in range(2):
            d[h].z_start(xs[k])

    lax.fori_loop(0, 4, multiply, 0)
    for part in (a, e):
        part[0].start(0, OPP_R, OPP_L)
    z_parts(2)
    lax.fori_loop(4, 7, multiply, 0)
    for part in (a, e):
        part[1].start(0, OPP_R, OPP_L)
    lax.fori_loop(7, 10, multiply, 0)
    a[0].start(0, NEAR_RB)
    z_parts(1)
    lax.fori_loop(10, 13, multiply, 0)
    a[0].start(0, NEAR_LA)
    a[0].relay(0)
    e[0].start(0, NEAR_RB, NEAR_LA)
    z_parts(3)
    lax.fori_loop(13, 16, multiply, 0)
    a[1].start(0, NEAR_RB, NEAR_LA)
    a[1].relay(0)
    e[1].start(0, NEAR_RB, NEAR_LA)
    z_parts(0)
    for h in range(2):
        a[h].gather(0)
        a[h].start(1, OPP_R, OPP_L, NEAR_RB, NEAR_LA)
    for h in range(2):
        e[h].relay(0)
    for h in range(2):
        a[h].relay(1)
    for h in range(2):
        e[h].gather(0)
        e[h].start(1, OPP_R, OPP_L, NEAR_RB, NEAR_LA)
    for h in range(2):
        b[h].start(0, OPP_R, OPP_L)
    for h in range(2):
        a[h].gather(1)
        a[h].z_start()
    for h in range(2):
        e[h].relay(1)
    for h in range(2):
        b[h].start(0, NEAR_RB, NEAR_LA)
    for h in range(2):
        e[h].gather(1)
        e[h].z_start()
    for h in range(2):
        b[h].relay(0)

    def climb(src, c, slot, sem, to):
        return pltpu.make_async_remote_copy(
            src_ref=src.at[c],
            dst_ref=stack.at[c, slot],
            send_sem=tree_send.at[sem, c],
            recv_sem=tree_recv.at[slot, c],
            device_id=device_of(to),
            device_id_type=pl.DeviceIdType.MESH,
        )

    for h in range(2):
        rows = jnp.concatenate([a[h].finish(), e[h].finish()], 0)
        for c in range(2 * h, 2 * h + 2):
            leaf_rows[c] = rows[:, (c - 2 * h) * PIECE : (c - 2 * h + 1) * PIECE]

            @pl.when(odd)
            def _():
                stack[c, 1] = leaf_rows[c]

            @pl.when(jnp.logical_not(odd))
            def _():
                climb(leaf_rows, c, 0, 0, me + 1).start()

    sends = level < LEVELS
    below_root = level == LEVELS - 1

    def tree(low, high):
        @pl.when(jnp.logical_and(level >= low, level <= high))
        def _():
            for c in range(PIECES):
                climb(leaf_rows, c, 0, 0, me + 1).wait_recv()

                @pl.when(jnp.logical_not(odd))
                def _():
                    climb(leaf_rows, c, 1, 0, me + 1).wait_recv()

                node_rows[c] = select(node_pick, stack[c].reshape(LR, PIECE))

                @pl.when(sends)
                def _():
                    climb(node_rows, c, side, 1, parent).start()

                @pl.when(below_root)
                def _():
                    climb(node_rows, c, side, 2, 0).start()

    def gram_of(rows):
        gram = 0.0
        for c in range(PIECES):
            gram = gram + times_transposed(rows[c], rows[c])
        return gram

    tree(1, 2)
    for h in range(2):
        b[h].gather(0)
        b[h].start(1, OPP_R, OPP_L, NEAR_RB, NEAR_LA)
    tree(3, 3)
    for h in range(2):
        b[h].relay(1)
    tree(4, 4)
    for h in range(2):
        d[h].z_merge(xs)
        d[h].start(0, OPP_R, OPP_L, NEAR_RB, NEAR_LA)
    tree(5, 5)
    for h in range(2):
        b[h].gather(1)
        b[h].z_start()
    for h in range(2):
        d[h].relay(0)
    tree(6, 6)
    for h in range(2):
        d[h].gather(0)
        d[h].start(1, OPP_R, OPP_L, NEAR_RB, NEAR_LA)
    tree(7, 7)
    for h in range(2):
        d[h].relay(1)
    leaf_inv, node_inv = inverses((gram_of(leaf_rows), gram_of(node_rows)))
    known = 0.0
    basis = 0.0
    for c in range(PIECES):
        weight = jnp.dot(leaf_inv, leaf_rows[c], precision=HIGHEST, preferred_element_type=F32)
        weights[c] = weight
        known = known + times_transposed(leaf_rows[c], weight)
        weight = jnp.dot(node_inv, node_rows[c], precision=HIGHEST, preferred_element_type=F32)
        basis = basis + times_transposed(stack[c].reshape(LR, PIECE), weight)
    node_out[0] = basis
    leaf_out[...] = select(unpick[:, :RANK].astype(BF16), known)

    found = []
    for part in (b, d):
        basis = 0.0
        for h in range(2):
            if part is d:
                part[h].gather(1)
            rows = part[h].finish()
            for c in range(2):
                basis = basis + times_transposed(
                    rows[:, c * PIECE : (c + 1) * PIECE], weights[2 * h + c]
                )
        found.append(basis)
    leaf_out[...] += select(unpick[:, RANK:].astype(BF16), jnp.concatenate(found, 0))

    for c in range(PIECES):

        @pl.when(jnp.logical_not(odd))
        def _():
            climb(leaf_rows, c, 0, 0, me + 1).wait_send()

        @pl.when(sends)
        def _():
            climb(node_rows, c, side, 1, parent).wait_send()

        @pl.when(below_root)
        def _():
            climb(node_rows, c, side, 2, 0).wait_send()

    lax.fori_loop(0, len(ORDER), share_sent, 0)
    for pair in halves:
        for half in pair:
            for copy in half.started:
                copy.wait_send()


def bases(matrix, probes, skel, node_skel):
    depth = probes.shape[0]
    scratch = [
        pltpu.VMEM((SLOTS, LR, depth), BF16),
        pltpu.VMEM((NZ, LR, depth), BF16),
        pltpu.VMEM((GROUP, 1, LR), F32),
        pltpu.VMEM((PIECES, RANK, PIECE), F32),
        pltpu.VMEM((PIECES, RANK, PIECE), F32),
        pltpu.VMEM((PIECES, 2, RANK, PIECE), F32),
        pltpu.VMEM((LR, LR), F32),
        pltpu.VMEM((PIECES, RANK, PIECE), F32),
        pltpu.SemaphoreType.DMA((SLOTS,)),
        pltpu.SemaphoreType.DMA((GROUP,)),
        pltpu.SemaphoreType.DMA((GROUP,)),
        pltpu.SemaphoreType.DMA((3, PIECES)),
        pltpu.SemaphoreType.DMA((2, PIECES)),
        pltpu.SemaphoreType.DMA((len(CHUNKS), 2, N_COPY)),
        pltpu.SemaphoreType.DMA((len(CHUNKS), 2, N_COPY)),
    ]
    for _, rows, z_first in CHUNKS:
        z = () if z_first else (NZ,)
        for _ in range(2):
            scratch += [
                pltpu.VMEM((NZ, 4, 4, rows, HALF) if z_first else (4, 4, NZ, rows, HALF), F32),
                pltpu.VMEM((2, 4, *z, rows // 2, HALF), F32),
                pltpu.VMEM((4, *z, rows, HALF), F32),
                pltpu.VMEM((4, *z, rows, HALF), F32),
                pltpu.VMEM((2, *z, rows // 2, HALF), F32),
                pltpu.VMEM((*z, rows, HALF), F32),
                pltpu.VMEM((*z, rows, HALF), F32),
                pltpu.VMEM((4, 4, rows, HALF) if z_first else (rows, HALF), F32),
            ]
    vmem = pl.BlockSpec(memory_space=pltpu.VMEM)
    return pl.pallas_call(
        kernel,
        out_shape=(
            jax.ShapeDtypeStruct((LR, RANK), F32),
            jax.ShapeDtypeStruct((1, LR, RANK), F32),
        ),
        in_specs=[pl.BlockSpec(memory_space=pl.ANY), vmem, vmem, vmem],
        out_specs=(vmem, vmem),
        scratch_shapes=scratch,
        compiler_params=pltpu.CompilerParams(
            collective_id=0, has_side_effects=True, vmem_limit_bytes=56 * 2**20
        ),
        name="bases",
    )(matrix, probes, skel, node_skel)


def on_device(matrix, probes, leaf_skeleton, node_skeleton):
    return bases(matrix, probes, leaf_skeleton, node_skeleton)


def solution(mesh):
    return jax.shard_map(
        on_device,
        mesh=mesh,
        in_specs=(P("grp", "leaf"), P("leaf", None), P(("grp", "leaf"), None), P()),
        out_specs=(P(("grp", "leaf"), None), P(("grp", "leaf"), None, None)),
        check_vma=False,
    )
```

```python
import jax
import jax.numpy as jnp
from jax import lax
from jax.experimental import pallas as pl
from jax.experimental.pallas import tpu as pltpu
from jax.sharding import PartitionSpec as P

NX, NY, NZ = 4, 4, 2
LR = 256
RANK = 128
HALF = 256
SLOTS = 8
CHUNKS = ((0, 64, False), (64, 64, False), (128, 64, False), (192, 64, True))
PIECES = 4
PIECE = 128
LEVELS = 7
GROUP = NX * NY * NZ
LEAVES = 128
PANEL = 16
AHEAD = 8
HIGHEST = lax.Precision.HIGHEST
F32 = jnp.float32
BF16 = jnp.bfloat16
ORDER = (
    [(2, 0), (2, 1), (2, 2), (2, 3)]
    + [(0, 2), (1, 2), (3, 2)]
    + [(1, 0), (1, 1), (1, 3)]
    + [(0, 1), (3, 1)]
    + [(3, 0), (3, 3)]
    + [(0, 3), (0, 0)]
)
OPP_R, OPP_L, NEAR_RA, NEAR_RB, NEAR_LA, NEAR_LB = range(6)
PASS = 6
Z_COPY = 2 * PASS
N_COPY = 2 * PASS + 12


def mod4(v):
    return lax.rem(v + 4, 4)


class Half:
    def __init__(self, part, bufs, zbuf, send, recv, rows, z_first, first, second, zh, dev):
        self.whole, self.bufs, self.zbuf = part, bufs, zbuf
        self.part = part.at[zh] if z_first else part
        self.send, self.recv = send, recv
        self.rows = rows
        self.z_first = z_first
        self.axes = (first, second)
        self.zh = zh
        self.dev = dev
        self.started = []
        self.pieces = False

    def block(self, phase, index):
        if phase == 0:
            return self.part.at[index]
        return self.part.at[self.axes[0][1], index]

    def lead(self, phase):
        return 2 - phase - self.z_first

    def begin(self, copy):
        copy.start()
        self.started.append(copy)

    def remote(self, src, dst, slot, to):
        return pltpu.make_async_remote_copy(
            src_ref=src,
            dst_ref=dst,
            send_sem=self.send.at[slot],
            recv_sem=self.recv.at[slot],
            device_id=to,
            device_id_type=pl.DeviceIdType.MESH,
        )

    def copy(self, phase, kind):
        name, me = self.axes[phase]
        half = self.rows // 2
        opp, near_r, near_l = self.bufs[phase]
        lo, hi = pl.ds(0, half), pl.ds(half, half)
        lead = (slice(None),) * self.lead(phase)
        right, left = mod4(me + 1), mod4(me - 1)
        index, rows, dst, to = {
            OPP_R: (mod4(me + 2), lo, opp.at[0], right),
            OPP_L: (mod4(me + 2), hi, opp.at[1], left),
            NEAR_RA: (right, lo, near_r.at[(*lead, lo)], right),
            NEAR_RB: (right, hi, near_r.at[(*lead, hi)], right),
            NEAR_LA: (left, lo, near_l.at[(*lead, lo)], left),
            NEAR_LB: (left, hi, near_l.at[(*lead, hi)], left),
        }[kind]
        return self.remote(
            self.block(phase, index).at[(*lead, rows)],
            dst,
            phase * PASS + kind,
            self.dev(**{name: to}),
        )

    def piece(self, kind, other):
        name, me = self.axes[0]
        half = self.rows // 2
        return self.remote(
            self.part.at[mod4(me + 2), other, :, pl.ds(kind * half, half)],
            self.bufs[0][0].at[kind, other],
            2 * PASS + 4 + 4 * kind + other,
            self.dev(**{name: mod4(me + 1) if kind == OPP_R else mod4(me - 1)}),
        )

    def piece_start(self, other):
        self.pieces = True
        for kind in (OPP_R, OPP_L):
            self.piece(kind, other).start()

    def start(self, phase, *kinds):
        for kind in kinds:
            self.begin(self.copy(phase, kind))

    def wait(self, phase, kind):
        if phase == 0 and self.pieces and kind in (OPP_R, OPP_L):
            for other in range(4):
                self.piece(kind, other).wait_recv()
        else:
            self.copy(phase, kind).wait_recv()

    def wait_sent(self):
        for copy in self.started:
            copy.wait_send()
        if self.pieces:
            for kind in (OPP_R, OPP_L):
                for other in range(4):
                    self.piece(kind, other).wait_send()

    def relay(self, phase):
        me = self.axes[phase][1]
        half = self.rows // 2
        opp = self.bufs[phase][0]
        for kind, side, index, row, on in (
            (OPP_R, 0, mod4(me + 1), 0, NEAR_RA),
            (OPP_L, 1, mod4(me - 1), half, NEAR_LB),
        ):
            self.wait(phase, kind)
            self.add(self.block(phase, index), phase, row, half, (opp.at[side],))
            self.start(phase, on)

    def gather(self, phase):
        me = self.axes[phase][1]
        for kind in (NEAR_RB, NEAR_LA, NEAR_RA, NEAR_LB):
            self.wait(phase, kind)
        self.add(self.block(phase, me), phase, 0, self.rows, self.bufs[phase][1:])

    def add(self, target, phase, row, count, terms):
        rows, term_rows = pl.ds(row, count), pl.ds(0, count)

        def step(at):
            value = target[(*at, rows)]
            for term in terms:
                value = value + term[(*at, term_rows)]
            target[(*at, rows)] = value

        if self.lead(phase) == 0:
            step(())
        elif self.lead(phase) == 1:
            lax.fori_loop(0, NZ if phase else 4, lambda i, c: (step((i,)), c)[1], 0)
        else:
            lax.fori_loop(0, 4 * NZ, lambda i, c: (step((i // NZ, lax.rem(i, NZ))), c)[1], 0)

    def z_copy(self, x=None):
        to = self.dev(z=1 - self.zh)
        if not self.z_first:
            src = self.part.at[self.axes[0][1], self.axes[1][1], 1 - self.zh]
            return self.remote(src, self.zbuf, 2 * PASS, to)
        steps, x = x
        at = (x,) if self.axes[0][0] == "x" else (slice(None), x)
        return self.remote(
            self.whole.at[(1 - self.zh, *at)], self.zbuf.at[at], 2 * PASS + steps, to
        )

    def z_start(self, x=None):
        self.begin(self.z_copy(x))

    def z_merge(self, xs):
        for x in xs:
            self.z_copy(x).wait_recv()

        def step(i, carry):
            at = (i // 4, lax.rem(i, 4))
            self.part[at] += self.zbuf[at]
            return carry

        lax.fori_loop(0, 16, step, 0)

    def finish(self):
        at = (self.axes[0][1], self.axes[1][1])
        if self.z_first:
            return self.part[at]
        self.z_copy().wait_recv()
        return self.part[(*at, self.zh)] + self.zbuf[...]


def leaf_order(skel):
    hit = (lax.broadcasted_iota(jnp.int32, (LR, RANK), 0) == skel).astype(F32).astype(BF16)
    picked = lax.dot_general(
        jnp.ones((8, RANK), BF16), hit, (((1,), (1,)), ((), ())), preferred_element_type=F32
    )
    before = (
        (
            lax.broadcasted_iota(jnp.int32, (LR, LR), 0)
            < lax.broadcasted_iota(jnp.int32, (LR, LR), 1)
        )
        .astype(F32)
        .astype(BF16)
    )
    count = jnp.dot(picked.astype(BF16), before, preferred_element_type=F32)
    lane = lax.broadcasted_iota(jnp.int32, (8, LR), 1).astype(F32)
    place = jnp.where(picked > 0.5, count, RANK + lane - count)
    return place[0:1]


def selection(place):
    return (lax.broadcasted_iota(jnp.int32, (LR, LR), 0).astype(F32) == place).astype(F32)


def select(pick, value):
    total = 0.0
    for _ in range(3):
        term = value.astype(BF16)
        total = total + jnp.dot(pick, term, preferred_element_type=F32)
        value = value - term.astype(F32)
    return total


def times_transposed(a, b):
    return lax.dot_general(
        a, b, (((1,), (1,)), ((), ())), precision=HIGHEST, preferred_element_type=F32
    )


def eliminate(panels):
    panels = list(panels)
    lane = lax.broadcasted_iota(jnp.int32, panels[0].shape, 1)
    sub = lax.broadcasted_iota(jnp.int32, panels[0].shape, 0)
    for base in range(0, PANEL, AHEAD):
        columns = [
            [jnp.broadcast_to(p[:, k : k + 1], p.shape) for k in range(base, base + AHEAD)]
            for p in panels
        ]
        for ahead in range(AHEAD):
            k = base + ahead
            for n, p in enumerate(panels):
                column = columns[n][ahead]
                scale = 1.0 / column[k : k + 1]
                row = jnp.where(lane[0:1] == k, 1.0, p[k : k + 1]) * scale
                rest = jnp.where(lane == k, 0.0, p) - column * row
                panels[n] = jnp.where(sub == k, row, rest)
                for later in range(ahead + 1, AHEAD):
                    other = columns[n][later]
                    row = other[k : k + 1] * scale
                    columns[n][later] = jnp.where(sub == k, row, other - column * row)
    return panels


def inverses(grams):
    def body(_, grams):
        panels = eliminate([g[:PANEL] for g in grams])
        done = []
        for g, p in zip(grams, panels):
            rest = g[PANEL:]
            lane = lax.broadcasted_iota(jnp.int32, rest.shape, 1)
            rest = jnp.where(lane < PANEL, 0.0, rest) - jnp.dot(
                rest[:, :PANEL], p, precision=HIGHEST, preferred_element_type=F32
            )
            done.append(pltpu.roll(jnp.concatenate([rest, p], 0), RANK - PANEL, 1))
        return tuple(done)

    return lax.fori_loop(0, RANK // PANEL, body, tuple(grams))


def kernel(
    matrix,
    probes,
    skel,
    node_skel,
    leaf_out,
    node_out,
    slots,
    permuted,
    places,
    leaf_rows,
    node_rows,
    stack,
    unpick,
    leaf_cross,
    in_sem,
    place_send,
    place_recv,
    tree_send,
    tree_recv,
    send,
    recv,
    *rest,
):
    leaf = lax.axis_index("leaf")
    grp = lax.axis_index("grp")
    x = lax.rem(leaf, NX)
    y = lax.rem(leaf // NX, NY)
    zh = leaf // (NX * NY)

    def dev(x=x, y=y, z=zh):
        return {"leaf": (z * NY + y) * NX + x}

    barrier = pltpu.get_barrier_semaphore()

    def peer(k):
        return {"leaf": lax.rem(leaf + k, GROUP)}

    def greet_peer(k, carry):
        pl.semaphore_signal(barrier, 1, device_id=peer(k), device_id_type=pl.DeviceIdType.MESH)
        return carry

    lax.fori_loop(1, GROUP, greet_peer, 0)

    me = grp * GROUP + leaf
    odd = lax.rem(me, 2) == 1
    level = jnp.int32(1)
    for k in range(1, LEVELS):
        level = jnp.where(lax.rem(me, 2**k) == 0, k + 1, level)
    step = sum(jnp.where(level == k, 2 ** (k - 1), 0) for k in range(1, LEVELS + 1))
    node = sum(
        jnp.where(level == k, LEAVES - (LEAVES >> (k - 1)) + me // 2**k, 0)
        for k in range(1, LEVELS + 1)
    )
    side = lax.rem(me // (2 * step), 2)
    parent = jnp.where(side == 0, me + step, me - step)
    top = me == 0

    def device_of(number):
        number = lax.rem(number + LEAVES, LEAVES)
        return {"grp": number // GROUP, "leaf": lax.rem(number, GROUP)}

    def greet(number):
        pl.semaphore_signal(
            barrier, 1, device_id=device_of(number), device_id_type=pl.DeviceIdType.MESH
        )

    @pl.when(odd)
    def _():
        greet(me - 1)

    @pl.when(jnp.logical_not(odd))
    def _():
        greet(jnp.where(top, LEAVES // 4, me - step // 2))
        greet(jnp.where(top, 3 * LEAVES // 4, me + step // 2))

    greeted = GROUP - 1 + jnp.where(odd, 0, 1)
    greeted = greeted + jnp.where(level < LEVELS, 1, 0) + jnp.where(level == LEVELS - 1, 1, 0)

    def steps_of(pair):
        i = sum(jnp.where(pair == k, o[0], 0) for k, o in enumerate(ORDER))
        j = sum(jnp.where(pair == k, o[1], 0) for k, o in enumerate(ORDER))
        return i, j

    def place_of(t):
        i, j = steps_of(t // NZ)
        return mod4(x + i), mod4(y + j), lax.rem(t, NZ)

    def load(t):
        xd, yd, zd = place_of(t)
        dest = (zd * NY + yd) * NX + xd
        slot = lax.rem(t, SLOTS)
        return pltpu.make_async_copy(
            matrix.at[pl.ds(pl.multiple_of(dest * LR, LR), LR), :],
            slots.at[slot],
            in_sem.at[slot],
        )

    def prefetch(t, carry):
        load(t).start()
        return carry

    lax.fori_loop(0, SLOTS, prefetch, 0)

    place = leaf_order(skel[...])
    places[leaf] = place
    pl.semaphore_wait(barrier, greeted)

    def share(pair, z):
        i, j = steps_of(pair)
        to = (z * NY + mod4(y - j)) * NX + mod4(x - i)
        copy = pltpu.make_async_remote_copy(
            src_ref=places.at[leaf],
            dst_ref=places.at[leaf],
            send_sem=place_send.at[NZ * pair + z],
            recv_sem=place_recv.at[NZ * pair + zh],
            device_id={"leaf": to},
            device_id_type=pl.DeviceIdType.MESH,
        )
        return to, copy

    def share_start(pair, carry):
        for z in range(NZ):
            to, copy = share(pair, z)
            pl.when(to != leaf)(copy.start)
        return carry

    def share_sent(pair, carry):
        for z in range(NZ):
            to, copy = share(pair, z)
            pl.when(to != leaf)(copy.wait_send)
        return carry

    def share_arrived(pair, z, dest):
        copy = pltpu.make_async_remote_copy(
            src_ref=places.at[dest],
            dst_ref=places.at[dest],
            send_sem=place_send.at[NZ * pair + z],
            recv_sem=place_recv.at[NZ * pair + z],
            device_id={"leaf": dest},
            device_id_type=pl.DeviceIdType.MESH,
        )
        pl.when(dest != leaf)(copy.wait_recv)

    lax.fori_loop(0, len(ORDER), share_start, 0)
    node_pick = selection(leaf_order(node_skel[pl.ds(node, 1), :]))[:RANK].astype(BF16)
    unpick[...] = selection(place).T

    halves = []
    rest = list(rest)
    parts = []
    for c, (_, rows, z_first) in enumerate(CHUNKS):
        pair = []
        for h in range(2):
            part, o1, r1, l1, o2, r2, l2, zb = rest[:8]
            rest = rest[8:]
            first, second = (("x", x), ("y", y)) if h == 0 else (("y", y), ("x", x))
            pair.append(
                Half(
                    part,
                    ((o1, r1, l1), (o2, r2, l2)),
                    zb,
                    send.at[c, h],
                    recv.at[c, h],
                    rows,
                    z_first,
                    first,
                    second,
                    zh,
                    dev,
                )
            )
        halves.append(pair)

    def multiply(pair, carry):
        i, j = steps_of(pair)
        xd, yd = mod4(x + i), mod4(y + j)
        rows_iota = lax.broadcasted_iota(jnp.int32, (LR, LR), 0).astype(F32)
        for zd in range(NZ):
            t = NZ * pair + zd
            dest = (zd * NY + yd) * NX + xd
            slot = lax.rem(t, SLOTS)
            load(t).wait()
            share_arrived(pair, zd, dest)
            pick = (rows_iota == places[dest]).astype(F32).astype(BF16)
            for block in range(probes.shape[0] // LR):
                cols = pl.ds(block * LR, LR)
                moved = jnp.dot(pick, slots[slot, :, cols], preferred_element_type=F32)
                own = leaf * (probes.shape[0] // LR) + block == grp * GROUP + dest
                permuted[zd, :, cols] = jnp.where(own, 0.0, moved).astype(BF16)
        for h in range(2):
            for zd in range(NZ):
                product = jnp.dot(
                    permuted[zd], probes[:, pl.ds(h * HALF, HALF)], preferred_element_type=F32
                )
                for c, (row, rows, z_first) in enumerate(CHUNKS):
                    at = (xd, yd) if h == 0 else (yd, xd)
                    at = (zd, *at) if z_first else (*at, zd)
                    halves[c][h].whole[at] = product[row : row + rows]

        @pl.when(NZ * pair + SLOTS < GROUP)
        def _():
            for zd in range(NZ):
                load(NZ * pair + zd + SLOTS).start()

        return carry

    a, e, b, d = halves
    xs = [(k, mod4(x + k)) for k in range(4)]

    def z_parts(k):
        for h in range(2):
            d[h].z_start(xs[k])

    def along_y(pair, carry):
        multiply(pair, carry)
        a[0].piece_start(mod4(y + steps_of(pair)[1]))
        return carry

    def along_x(pair, carry):
        multiply(pair, carry)
        a[1].piece_start(mod4(x + steps_of(pair)[0]))
        return carry

    lax.fori_loop(0, 4, along_y, 0)
    e[0].start(0, OPP_R, OPP_L)
    a[1].piece_start(mod4(x + 2))
    z_parts(2)
    lax.fori_loop(4, 7, along_x, 0)
    e[1].start(0, OPP_R, OPP_L)
    lax.fori_loop(7, 10, multiply, 0)
    a[0].start(0, NEAR_RB)
    z_parts(1)
    lax.fori_loop(10, 12, multiply, 0)
    a[1].start(0, NEAR_RB)
    lax.fori_loop(12, 14, multiply, 0)
    a[0].start(0, NEAR_LA)
    a[0].relay(0)
    e[0].start(0, NEAR_RB, NEAR_LA)
    z_parts(3)
    lax.fori_loop(14, 16, multiply, 0)
    a[1].start(0, NEAR_LA)
    a[1].relay(0)
    e[1].start(0, NEAR_RB, NEAR_LA)
    z_parts(0)
    for h in range(2):
        a[h].gather(0)
        a[h].start(1, OPP_R, OPP_L, NEAR_RB, NEAR_LA)
    for h in range(2):
        e[h].relay(0)
    for h in range(2):
        a[h].relay(1)
    for h in range(2):
        e[h].gather(0)
        e[h].start(1, OPP_R, OPP_L, NEAR_RB, NEAR_LA)
    for h in range(2):
        b[h].start(0, OPP_R, OPP_L)
    for h in range(2):
        a[h].gather(1)
        a[h].z_start()
    for h in range(2):
        e[h].relay(1)
    for h in range(2):
        b[h].start(0, NEAR_RB, NEAR_LA)
    for h in range(2):
        e[h].gather(1)
        e[h].z_start()
    for h in range(2):
        b[h].relay(0)

    def climb(src, c, slot, sem, to):
        return pltpu.make_async_remote_copy(
            src_ref=src.at[c],
            dst_ref=stack.at[c, slot],
            send_sem=tree_send.at[sem, c],
            recv_sem=tree_recv.at[slot, c],
            device_id=device_of(to),
            device_id_type=pl.DeviceIdType.MESH,
        )

    for h in range(2):
        rows = jnp.concatenate([a[h].finish(), e[h].finish()], 0)
        for c in range(2 * h, 2 * h + 2):
            leaf_rows[c] = rows[:, (c - 2 * h) * PIECE : (c - 2 * h + 1) * PIECE]

            @pl.when(odd)
            def _():
                stack[c, 1] = leaf_rows[c]

            @pl.when(jnp.logical_not(odd))
            def _():
                climb(leaf_rows, c, 0, 0, me + 1).start()

    sends = level < LEVELS
    below_root = level == LEVELS - 1

    def tree(low, high):
        @pl.when(jnp.logical_and(level >= low, level <= high))
        def _():
            for c in range(PIECES):
                climb(leaf_rows, c, 0, 0, me + 1).wait_recv()

                @pl.when(jnp.logical_not(odd))
                def _():
                    climb(leaf_rows, c, 1, 0, me + 1).wait_recv()

                node_rows[c] = select(node_pick, stack[c].reshape(LR, PIECE))

                @pl.when(sends)
                def _():
                    climb(node_rows, c, side, 1, parent).start()

                @pl.when(below_root)
                def _():
                    climb(node_rows, c, side, 2, 0).start()

    def cross_of(rows, against):
        cross = 0.0
        for c in range(PIECES):
            cross = cross + times_transposed(rows(c), against[c])
        return cross

    def add_crosses(row, parts):
        crosses = []
        for part in parts:
            halves = [part[h].finish() for h in range(2)]
            crosses.append(
                cross_of(
                    lambda c: halves[c // 2][:, (c % 2) * PIECE : (c % 2 + 1) * PIECE], leaf_rows
                )
            )
        cross = jnp.concatenate(crosses, 0)
        pick = unpick[:, row : row + cross.shape[0]].astype(BF16)
        leaf_cross[...] += select(pick, cross)

    first_all = (OPP_R, OPP_L, NEAR_RB, NEAR_LA)
    tree(1, 1)
    d[1].z_merge(xs)
    d[1].start(0, *first_all)
    tree(2, 2)
    for h in range(2):
        b[h].gather(0)
        b[h].start(1, *first_all)
    d[1].relay(0)
    tree(3, 3)
    for h in range(2):
        b[h].relay(1)
    d[0].z_merge(xs)
    d[0].start(0, *first_all)
    d[1].gather(0)
    d[1].start(1, *first_all)
    tree(4, 4)
    d[0].relay(0)
    for h in range(2):
        b[h].gather(1)
        b[h].z_start()
    tree(5, 5)
    d[1].relay(1)
    d[0].gather(0)
    d[0].start(1, *first_all)
    tree(6, 6)
    d[0].relay(1)
    leaf_gram = cross_of(lambda c: leaf_rows[c], leaf_rows)
    leaf_cross[...] = select(unpick[:, :RANK].astype(BF16), leaf_gram)
    tree(7, 7)
    node_cross = cross_of(lambda c: stack[c].reshape(LR, PIECE), node_rows)
    node_gram = select(node_pick, node_cross)
    for h in range(2):
        d[h].gather(1)
    add_crosses(RANK, (b, d))
    leaf_inv, node_inv = inverses((leaf_gram, node_gram))
    node_out[0] = jnp.dot(node_cross, node_inv, precision=HIGHEST, preferred_element_type=F32)
    leaf_out[...] = jnp.dot(
        leaf_cross[...], leaf_inv, precision=HIGHEST, preferred_element_type=F32
    )

    for c in range(PIECES):

        @pl.when(jnp.logical_not(odd))
        def _():
            climb(leaf_rows, c, 0, 0, me + 1).wait_send()

        @pl.when(sends)
        def _():
            climb(node_rows, c, side, 1, parent).wait_send()

        @pl.when(below_root)
        def _():
            climb(node_rows, c, side, 2, 0).wait_send()

    lax.fori_loop(0, len(ORDER), share_sent, 0)
    for pair in halves:
        for half in pair:
            half.wait_sent()


def bases(matrix, probes, skel, node_skel):
    depth = probes.shape[0]
    scratch = [
        pltpu.VMEM((SLOTS, LR, depth), BF16),
        pltpu.VMEM((NZ, LR, depth), BF16),
        pltpu.VMEM((GROUP, 1, LR), F32),
        pltpu.VMEM((PIECES, RANK, PIECE), F32),
        pltpu.VMEM((PIECES, RANK, PIECE), F32),
        pltpu.VMEM((PIECES, 2, RANK, PIECE), F32),
        pltpu.VMEM((LR, LR), F32),
        pltpu.VMEM((LR, RANK), F32),
        pltpu.SemaphoreType.DMA((SLOTS,)),
        pltpu.SemaphoreType.DMA((GROUP,)),
        pltpu.SemaphoreType.DMA((GROUP,)),
        pltpu.SemaphoreType.DMA((3, PIECES)),
        pltpu.SemaphoreType.DMA((2, PIECES)),
        pltpu.SemaphoreType.DMA((len(CHUNKS), 2, N_COPY)),
        pltpu.SemaphoreType.DMA((len(CHUNKS), 2, N_COPY)),
    ]
    for _, rows, z_first in CHUNKS:
        z = () if z_first else (NZ,)
        for _ in range(2):
            scratch += [
                pltpu.VMEM((NZ, 4, 4, rows, HALF) if z_first else (4, 4, NZ, rows, HALF), F32),
                pltpu.VMEM((2, 4, *z, rows // 2, HALF), F32),
                pltpu.VMEM((4, *z, rows, HALF), F32),
                pltpu.VMEM((4, *z, rows, HALF), F32),
                pltpu.VMEM((2, *z, rows // 2, HALF), F32),
                pltpu.VMEM((*z, rows, HALF), F32),
                pltpu.VMEM((*z, rows, HALF), F32),
                pltpu.VMEM((4, 4, rows, HALF) if z_first else (rows, HALF), F32),
            ]
    vmem = pl.BlockSpec(memory_space=pltpu.VMEM)
    return pl.pallas_call(
        kernel,
        out_shape=(
            jax.ShapeDtypeStruct((LR, RANK), F32),
            jax.ShapeDtypeStruct((1, LR, RANK), F32),
        ),
        in_specs=[pl.BlockSpec(memory_space=pl.ANY), vmem, vmem, vmem],
        out_specs=(vmem, vmem),
        scratch_shapes=scratch,
        compiler_params=pltpu.CompilerParams(
            collective_id=0, has_side_effects=True, vmem_limit_bytes=56 * 2**20
        ),
        name="bases",
    )(matrix, probes, skel, node_skel)


def on_device(matrix, probes, leaf_skeleton, node_skeleton):
    return bases(matrix, probes, leaf_skeleton, node_skeleton)


def solution(mesh):
    return jax.shard_map(
        on_device,
        mesh=mesh,
        in_specs=(P("grp", "leaf"), P("leaf", None), P(("grp", "leaf"), None), P()),
        out_specs=(P(("grp", "leaf"), None), P(("grp", "leaf"), None, None)),
        check_vma=False,
    )
```

```python
import jax
import jax.numpy as jnp
from jax import lax
from jax.experimental import pallas as pl
from jax.experimental.pallas import tpu as pltpu
from jax.sharding import PartitionSpec as P

NX, NY, NZ = 4, 4, 2
LR = 256
RANK = 128
HALF = 256
SLOTS = 8
CHUNKS = ((0, 64, False), (64, 64, False), (128, 64, False), (192, 64, True))
PIECES = 4
PIECE = 128
LEVELS = 7
GROUP = NX * NY * NZ
LEAVES = 128
PANEL = 16
AHEAD = 8
HIGHEST = lax.Precision.HIGHEST
F32 = jnp.float32
BF16 = jnp.bfloat16
ORDER = (
    [(2, 0), (2, 1), (2, 2), (2, 3)]
    + [(0, 2), (1, 2), (3, 2)]
    + [(1, 0), (1, 1), (1, 3)]
    + [(0, 1), (3, 1)]
    + [(3, 0), (3, 3)]
    + [(0, 3), (0, 0)]
)
OPP_R, OPP_L, NEAR_RA, NEAR_RB, NEAR_LA, NEAR_LB = range(6)
PASS = 6
Z_COPY = 2 * PASS
N_COPY = 2 * PASS + 12


def mod4(v):
    return lax.rem(v + 4, 4)


class Half:
    def __init__(self, part, bufs, zbuf, send, recv, rows, z_first, first, second, zh, dev):
        self.whole, self.bufs, self.zbuf = part, bufs, zbuf
        self.part = part.at[zh] if z_first else part
        self.send, self.recv = send, recv
        self.rows = rows
        self.z_first = z_first
        self.axes = (first, second)
        self.zh = zh
        self.dev = dev
        self.started = []
        self.pieces = False

    def block(self, phase, index):
        if phase == 0:
            return self.part.at[index]
        return self.part.at[self.axes[0][1], index]

    def lead(self, phase):
        return 2 - phase - self.z_first

    def begin(self, copy):
        copy.start()
        self.started.append(copy)

    def remote(self, src, dst, slot, to):
        return pltpu.make_async_remote_copy(
            src_ref=src,
            dst_ref=dst,
            send_sem=self.send.at[slot],
            recv_sem=self.recv.at[slot],
            device_id=to,
            device_id_type=pl.DeviceIdType.MESH,
        )

    def copy(self, phase, kind):
        name, me = self.axes[phase]
        half = self.rows // 2
        opp, near_r, near_l = self.bufs[phase]
        lo, hi = pl.ds(0, half), pl.ds(half, half)
        lead = (slice(None),) * self.lead(phase)
        right, left = mod4(me + 1), mod4(me - 1)
        index, rows, dst, to = {
            OPP_R: (mod4(me + 2), lo, opp.at[0], right),
            OPP_L: (mod4(me + 2), hi, opp.at[1], left),
            NEAR_RA: (right, lo, near_r.at[(*lead, lo)], right),
            NEAR_RB: (right, hi, near_r.at[(*lead, hi)], right),
            NEAR_LA: (left, lo, near_l.at[(*lead, lo)], left),
            NEAR_LB: (left, hi, near_l.at[(*lead, hi)], left),
        }[kind]
        return self.remote(
            self.block(phase, index).at[(*lead, rows)],
            dst,
            phase * PASS + kind,
            self.dev(**{name: to}),
        )

    def piece(self, kind, other):
        name, me = self.axes[0]
        half = self.rows // 2
        return self.remote(
            self.part.at[mod4(me + 2), other, :, pl.ds(kind * half, half)],
            self.bufs[0][0].at[kind, other],
            2 * PASS + 4 + 4 * kind + other,
            self.dev(**{name: mod4(me + 1) if kind == OPP_R else mod4(me - 1)}),
        )

    def piece_start(self, other):
        self.pieces = True
        for kind in (OPP_R, OPP_L):
            self.piece(kind, other).start()

    def start(self, phase, *kinds):
        for kind in kinds:
            self.begin(self.copy(phase, kind))

    def wait(self, phase, kind):
        if phase == 0 and self.pieces and kind in (OPP_R, OPP_L):
            for other in range(4):
                self.piece(kind, other).wait_recv()
        else:
            self.copy(phase, kind).wait_recv()

    def wait_sent(self):
        for copy in self.started:
            copy.wait_send()
        if self.pieces:
            for kind in (OPP_R, OPP_L):
                for other in range(4):
                    self.piece(kind, other).wait_send()

    def relay(self, phase):
        me = self.axes[phase][1]
        half = self.rows // 2
        opp = self.bufs[phase][0]
        for kind, side, index, row, on in (
            (OPP_R, 0, mod4(me + 1), 0, NEAR_RA),
            (OPP_L, 1, mod4(me - 1), half, NEAR_LB),
        ):
            self.wait(phase, kind)
            self.add(self.block(phase, index), phase, row, half, (opp.at[side],))
            self.start(phase, on)

    def gather(self, phase):
        me = self.axes[phase][1]
        for kind in (NEAR_RB, NEAR_LA, NEAR_RA, NEAR_LB):
            self.wait(phase, kind)
        self.add(self.block(phase, me), phase, 0, self.rows, self.bufs[phase][1:])

    def add(self, target, phase, row, count, terms):
        rows, term_rows = pl.ds(row, count), pl.ds(0, count)

        def step(at):
            value = target[(*at, rows)]
            for term in terms:
                value = value + term[(*at, term_rows)]
            target[(*at, rows)] = value

        if self.lead(phase) == 0:
            step(())
        elif self.lead(phase) == 1:
            lax.fori_loop(0, NZ if phase else 4, lambda i, c: (step((i,)), c)[1], 0)
        else:
            lax.fori_loop(0, 4 * NZ, lambda i, c: (step((i // NZ, lax.rem(i, NZ))), c)[1], 0)

    def z_copy(self, x=None):
        to = self.dev(z=1 - self.zh)
        if not self.z_first:
            src = self.part.at[self.axes[0][1], self.axes[1][1], 1 - self.zh]
            return self.remote(src, self.zbuf, 2 * PASS, to)
        steps, x = x
        at = (x,) if self.axes[0][0] == "x" else (slice(None), x)
        return self.remote(
            self.whole.at[(1 - self.zh, *at)], self.zbuf.at[at], 2 * PASS + steps, to
        )

    def z_start(self, x=None):
        self.begin(self.z_copy(x))

    def z_merge(self, xs):
        for x in xs:
            self.z_copy(x).wait_recv()

        def step(i, carry):
            at = (i // 4, lax.rem(i, 4))
            self.part[at] += self.zbuf[at]
            return carry

        lax.fori_loop(0, 16, step, 0)

    def finish(self):
        at = (self.axes[0][1], self.axes[1][1])
        if self.z_first:
            return self.part[at]
        self.z_copy().wait_recv()
        return self.part[(*at, self.zh)] + self.zbuf[...]


def leaf_order(skel):
    hit = (lax.broadcasted_iota(jnp.int32, (LR, RANK), 0) == skel).astype(F32).astype(BF16)
    picked = lax.dot_general(
        jnp.ones((8, RANK), BF16), hit, (((1,), (1,)), ((), ())), preferred_element_type=F32
    )
    before = (
        (
            lax.broadcasted_iota(jnp.int32, (LR, LR), 0)
            < lax.broadcasted_iota(jnp.int32, (LR, LR), 1)
        )
        .astype(F32)
        .astype(BF16)
    )
    count = jnp.dot(picked.astype(BF16), before, preferred_element_type=F32)
    lane = lax.broadcasted_iota(jnp.int32, (8, LR), 1).astype(F32)
    place = jnp.where(picked > 0.5, count, RANK + lane - count)
    return place[0:1]


def selection(place):
    return (lax.broadcasted_iota(jnp.int32, (LR, LR), 0).astype(F32) == place).astype(F32)


def select(pick, value):
    total = 0.0
    for _ in range(3):
        term = value.astype(BF16)
        total = total + jnp.dot(pick, term, preferred_element_type=F32)
        value = value - term.astype(F32)
    return total


def times_transposed(a, b):
    return lax.dot_general(
        a, b, (((1,), (1,)), ((), ())), precision=HIGHEST, preferred_element_type=F32
    )


def eliminate(panels):
    panels = list(panels)
    lane = lax.broadcasted_iota(jnp.int32, panels[0].shape, 1)
    sub = lax.broadcasted_iota(jnp.int32, panels[0].shape, 0)
    for base in range(0, PANEL, AHEAD):
        columns = [
            [jnp.broadcast_to(p[:, k : k + 1], p.shape) for k in range(base, base + AHEAD)]
            for p in panels
        ]
        for ahead in range(AHEAD):
            k = base + ahead
            for n, p in enumerate(panels):
                column = columns[n][ahead]
                scale = 1.0 / column[k : k + 1]
                row = jnp.where(lane[0:1] == k, 1.0, p[k : k + 1]) * scale
                rest = jnp.where(lane == k, 0.0, p) - column * row
                panels[n] = jnp.where(sub == k, row, rest)
                for later in range(ahead + 1, AHEAD):
                    other = columns[n][later]
                    row = other[k : k + 1] * scale
                    columns[n][later] = jnp.where(sub == k, row, other - column * row)
    return panels


def inverses(grams):
    def body(_, grams):
        panels = eliminate([g[:PANEL] for g in grams])
        done = []
        for g, p in zip(grams, panels):
            rest = g[PANEL:]
            lane = lax.broadcasted_iota(jnp.int32, rest.shape, 1)
            rest = jnp.where(lane < PANEL, 0.0, rest) - jnp.dot(
                rest[:, :PANEL], p, precision=HIGHEST, preferred_element_type=F32
            )
            done.append(pltpu.roll(jnp.concatenate([rest, p], 0), RANK - PANEL, 1))
        return tuple(done)

    return lax.fori_loop(0, RANK // PANEL, body, tuple(grams))


def kernel(
    matrix,
    probes,
    skel,
    node_skel,
    leaf_out,
    node_out,
    slots,
    permuted,
    places,
    leaf_rows,
    node_rows,
    stack,
    unpick,
    leaf_cross,
    in_sem,
    place_send,
    place_recv,
    tree_send,
    tree_recv,
    send,
    recv,
    *rest,
):
    leaf = lax.axis_index("leaf")
    grp = lax.axis_index("grp")
    x = lax.rem(leaf, NX)
    y = lax.rem(leaf // NX, NY)
    zh = leaf // (NX * NY)

    def dev(x=x, y=y, z=zh):
        return {"leaf": (z * NY + y) * NX + x}

    barrier = pltpu.get_barrier_semaphore()

    def peer(k):
        return {"leaf": lax.rem(leaf + k, GROUP)}

    def greet_peer(k, carry):
        pl.semaphore_signal(barrier, 1, device_id=peer(k), device_id_type=pl.DeviceIdType.MESH)
        return carry

    lax.fori_loop(1, GROUP, greet_peer, 0)

    me = grp * GROUP + leaf
    odd = lax.rem(me, 2) == 1
    level = jnp.int32(1)
    for k in range(1, LEVELS):
        level = jnp.where(lax.rem(me, 2**k) == 0, k + 1, level)
    step = sum(jnp.where(level == k, 2 ** (k - 1), 0) for k in range(1, LEVELS + 1))
    node = sum(
        jnp.where(level == k, LEAVES - (LEAVES >> (k - 1)) + me // 2**k, 0)
        for k in range(1, LEVELS + 1)
    )
    side = lax.rem(me // (2 * step), 2)
    parent = jnp.where(side == 0, me + step, me - step)
    top = me == 0

    def device_of(number):
        number = lax.rem(number + LEAVES, LEAVES)
        return {"grp": number // GROUP, "leaf": lax.rem(number, GROUP)}

    def greet(number):
        pl.semaphore_signal(
            barrier, 1, device_id=device_of(number), device_id_type=pl.DeviceIdType.MESH
        )

    @pl.when(odd)
    def _():
        greet(me - 1)

    @pl.when(jnp.logical_not(odd))
    def _():
        greet(jnp.where(top, LEAVES // 4, me - step // 2))
        greet(jnp.where(top, 3 * LEAVES // 4, me + step // 2))

    greeted = GROUP - 1 + jnp.where(odd, 0, 1)
    greeted = greeted + jnp.where(level < LEVELS, 1, 0) + jnp.where(level == LEVELS - 1, 1, 0)

    def steps_of(pair):
        i = sum(jnp.where(pair == k, o[0], 0) for k, o in enumerate(ORDER))
        j = sum(jnp.where(pair == k, o[1], 0) for k, o in enumerate(ORDER))
        return i, j

    def place_of(t):
        i, j = steps_of(t // NZ)
        return mod4(x + i), mod4(y + j), lax.rem(t, NZ)

    def load(t):
        xd, yd, zd = place_of(t)
        dest = (zd * NY + yd) * NX + xd
        slot = lax.rem(t, SLOTS)
        return pltpu.make_async_copy(
            matrix.at[pl.ds(pl.multiple_of(dest * LR, LR), LR), :],
            slots.at[slot],
            in_sem.at[slot],
        )

    def prefetch(t, carry):
        load(t).start()
        return carry

    lax.fori_loop(0, SLOTS, prefetch, 0)

    place = leaf_order(skel[...])
    places[leaf] = place
    pl.semaphore_wait(barrier, greeted)

    def share(pair, z):
        i, j = steps_of(pair)
        to = (z * NY + mod4(y - j)) * NX + mod4(x - i)
        copy = pltpu.make_async_remote_copy(
            src_ref=places.at[leaf],
            dst_ref=places.at[leaf],
            send_sem=place_send.at[NZ * pair + z],
            recv_sem=place_recv.at[NZ * pair + zh],
            device_id={"leaf": to},
            device_id_type=pl.DeviceIdType.MESH,
        )
        return to, copy

    def share_start(pair, carry):
        for z in range(NZ):
            to, copy = share(pair, z)
            pl.when(to != leaf)(copy.start)
        return carry

    def share_sent(pair, carry):
        for z in range(NZ):
            to, copy = share(pair, z)
            pl.when(to != leaf)(copy.wait_send)
        return carry

    def share_arrived(pair, z, dest):
        copy = pltpu.make_async_remote_copy(
            src_ref=places.at[dest],
            dst_ref=places.at[dest],
            send_sem=place_send.at[NZ * pair + z],
            recv_sem=place_recv.at[NZ * pair + z],
            device_id={"leaf": dest},
            device_id_type=pl.DeviceIdType.MESH,
        )
        pl.when(dest != leaf)(copy.wait_recv)

    lax.fori_loop(0, len(ORDER), share_start, 0)
    node_pick = selection(leaf_order(node_skel[pl.ds(node, 1), :]))[:RANK].astype(BF16)
    unpick[...] = selection(place).T

    halves = []
    rest = list(rest)
    parts = []
    for c, (_, rows, z_first) in enumerate(CHUNKS):
        pair = []
        for h in range(2):
            part, o1, r1, l1, o2, r2, l2, zb = rest[:8]
            rest = rest[8:]
            first, second = (("x", x), ("y", y)) if h == 0 else (("y", y), ("x", x))
            pair.append(
                Half(
                    part,
                    ((o1, r1, l1), (o2, r2, l2)),
                    zb,
                    send.at[c, h],
                    recv.at[c, h],
                    rows,
                    z_first,
                    first,
                    second,
                    zh,
                    dev,
                )
            )
        halves.append(pair)

    def multiply(pair, carry):
        i, j = steps_of(pair)
        xd, yd = mod4(x + i), mod4(y + j)
        rows_iota = lax.broadcasted_iota(jnp.int32, (LR, LR), 0).astype(F32)
        for zd in range(NZ):
            t = NZ * pair + zd
            dest = (zd * NY + yd) * NX + xd
            slot = lax.rem(t, SLOTS)
            load(t).wait()
            share_arrived(pair, zd, dest)
            pick = (rows_iota == places[dest]).astype(F32).astype(BF16)
            for block in range(probes.shape[0] // LR):
                cols = pl.ds(block * LR, LR)
                moved = jnp.dot(pick, slots[slot, :, cols], preferred_element_type=F32)
                own = leaf * (probes.shape[0] // LR) + block == grp * GROUP + dest
                permuted[pl.ds(zd * LR, LR), cols] = jnp.where(own, 0.0, moved).astype(BF16)
        for h in range(2):
            product = jnp.dot(
                permuted[...], probes[:, pl.ds(h * HALF, HALF)], preferred_element_type=F32
            )
            for zd in range(NZ):
                for c, (row, rows, z_first) in enumerate(CHUNKS):
                    at = (xd, yd) if h == 0 else (yd, xd)
                    at = (zd, *at) if z_first else (*at, zd)
                    row += zd * LR
                    halves[c][h].whole[at] = product[row : row + rows]

        @pl.when(NZ * pair + SLOTS < GROUP)
        def _():
            for zd in range(NZ):
                load(NZ * pair + zd + SLOTS).start()

        return carry

    a, e, b, d = halves
    xs = [(k, mod4(x + k)) for k in range(4)]

    def z_parts(k):
        for h in range(2):
            d[h].z_start(xs[k])

    def along_y(pair, carry):
        multiply(pair, carry)
        a[0].piece_start(mod4(y + steps_of(pair)[1]))
        return carry

    def along_x(pair, carry):
        multiply(pair, carry)
        a[1].piece_start(mod4(x + steps_of(pair)[0]))
        return carry

    lax.fori_loop(0, 4, along_y, 0)
    e[0].start(0, OPP_R, OPP_L)
    a[1].piece_start(mod4(x + 2))
    z_parts(2)
    lax.fori_loop(4, 7, along_x, 0)
    e[1].start(0, OPP_R, OPP_L)
    lax.fori_loop(7, 10, multiply, 0)
    a[0].start(0, NEAR_RB)
    z_parts(1)
    lax.fori_loop(10, 12, multiply, 0)
    a[1].start(0, NEAR_RB)
    lax.fori_loop(12, 14, multiply, 0)
    a[0].start(0, NEAR_LA)
    a[0].relay(0)
    e[0].start(0, NEAR_RB, NEAR_LA)
    z_parts(3)
    lax.fori_loop(14, 16, multiply, 0)
    a[1].start(0, NEAR_LA)
    a[1].relay(0)
    e[1].start(0, NEAR_RB, NEAR_LA)
    z_parts(0)
    for h in range(2):
        a[h].gather(0)
        a[h].start(1, OPP_R, OPP_L, NEAR_RB, NEAR_LA)
    for h in range(2):
        e[h].relay(0)
    for h in range(2):
        a[h].relay(1)
    for h in range(2):
        e[h].gather(0)
        e[h].start(1, OPP_R, OPP_L, NEAR_RB, NEAR_LA)
    for h in range(2):
        b[h].start(0, OPP_R, OPP_L)
    for h in range(2):
        a[h].gather(1)
        a[h].z_start()
    for h in range(2):
        e[h].relay(1)
    for h in range(2):
        b[h].start(0, NEAR_RB, NEAR_LA)
    for h in range(2):
        e[h].gather(1)
        e[h].z_start()
    for h in range(2):
        b[h].relay(0)

    def climb(src, c, slot, sem, to):
        return pltpu.make_async_remote_copy(
            src_ref=src.at[c],
            dst_ref=stack.at[c, slot],
            send_sem=tree_send.at[sem, c],
            recv_sem=tree_recv.at[slot, c],
            device_id=device_of(to),
            device_id_type=pl.DeviceIdType.MESH,
        )

    for h in range(2):
        rows = jnp.concatenate([a[h].finish(), e[h].finish()], 0)
        for c in range(2 * h, 2 * h + 2):
            leaf_rows[c] = rows[:, (c - 2 * h) * PIECE : (c - 2 * h + 1) * PIECE]

            @pl.when(odd)
            def _():
                stack[c, 1] = leaf_rows[c]

            @pl.when(jnp.logical_not(odd))
            def _():
                climb(leaf_rows, c, 0, 0, me + 1).start()

    sends = level < LEVELS
    below_root = level == LEVELS - 1

    def tree(low, high):
        @pl.when(jnp.logical_and(level >= low, level <= high))
        def _():
            for c in range(PIECES):
                climb(leaf_rows, c, 0, 0, me + 1).wait_recv()

                @pl.when(jnp.logical_not(odd))
                def _():
                    climb(leaf_rows, c, 1, 0, me + 1).wait_recv()

                node_rows[c] = select(node_pick, stack[c].reshape(LR, PIECE))

                @pl.when(sends)
                def _():
                    climb(node_rows, c, side, 1, parent).start()

                @pl.when(below_root)
                def _():
                    climb(node_rows, c, side, 2, 0).start()

    def cross_of(rows, against):
        cross = 0.0
        for c in range(PIECES):
            cross = cross + times_transposed(rows(c), against[c])
        return cross

    def add_crosses(row, parts):
        crosses = []
        for part in parts:
            halves = [part[h].finish() for h in range(2)]
            crosses.append(
                cross_of(
                    lambda c: halves[c // 2][:, (c % 2) * PIECE : (c % 2 + 1) * PIECE], leaf_rows
                )
            )
        cross = jnp.concatenate(crosses, 0)
        pick = unpick[:, row : row + cross.shape[0]].astype(BF16)
        leaf_cross[...] += select(pick, cross)

    first_all = (OPP_R, OPP_L, NEAR_RB, NEAR_LA)
    tree(1, 1)
    d[1].z_merge(xs)
    d[1].start(0, *first_all)
    tree(2, 2)
    for h in range(2):
        b[h].gather(0)
        b[h].start(1, *first_all)
    d[1].relay(0)
    tree(3, 3)
    for h in range(2):
        b[h].relay(1)
    d[0].z_merge(xs)
    d[0].start(0, *first_all)
    d[1].gather(0)
    d[1].start(1, *first_all)
    tree(4, 4)
    d[0].relay(0)
    for h in range(2):
        b[h].gather(1)
        b[h].z_start()
    tree(5, 5)
    d[1].relay(1)
    d[0].gather(0)
    d[0].start(1, *first_all)
    tree(6, 6)
    d[0].relay(1)
    leaf_gram = cross_of(lambda c: leaf_rows[c], leaf_rows)
    leaf_cross[...] = select(unpick[:, :RANK].astype(BF16), leaf_gram)
    tree(7, 7)
    node_cross = cross_of(lambda c: stack[c].reshape(LR, PIECE), node_rows)
    node_gram = select(node_pick, node_cross)
    for h in range(2):
        d[h].gather(1)
    add_crosses(RANK, (b, d))
    leaf_inv, node_inv = inverses((leaf_gram, node_gram))
    node_out[0] = jnp.dot(node_cross, node_inv, precision=HIGHEST, preferred_element_type=F32)
    leaf_out[...] = jnp.dot(
        leaf_cross[...], leaf_inv, precision=HIGHEST, preferred_element_type=F32
    )

    for c in range(PIECES):

        @pl.when(jnp.logical_not(odd))
        def _():
            climb(leaf_rows, c, 0, 0, me + 1).wait_send()

        @pl.when(sends)
        def _():
            climb(node_rows, c, side, 1, parent).wait_send()

        @pl.when(below_root)
        def _():
            climb(node_rows, c, side, 2, 0).wait_send()

    lax.fori_loop(0, len(ORDER), share_sent, 0)
    for pair in halves:
        for half in pair:
            half.wait_sent()


def bases(matrix, probes, skel, node_skel):
    depth = probes.shape[0]
    scratch = [
        pltpu.VMEM((SLOTS, LR, depth), BF16),
        pltpu.VMEM((NZ * LR, depth), BF16),
        pltpu.VMEM((GROUP, 1, LR), F32),
        pltpu.VMEM((PIECES, RANK, PIECE), F32),
        pltpu.VMEM((PIECES, RANK, PIECE), F32),
        pltpu.VMEM((PIECES, 2, RANK, PIECE), F32),
        pltpu.VMEM((LR, LR), F32),
        pltpu.VMEM((LR, RANK), F32),
        pltpu.SemaphoreType.DMA((SLOTS,)),
        pltpu.SemaphoreType.DMA((GROUP,)),
        pltpu.SemaphoreType.DMA((GROUP,)),
        pltpu.SemaphoreType.DMA((3, PIECES)),
        pltpu.SemaphoreType.DMA((2, PIECES)),
        pltpu.SemaphoreType.DMA((len(CHUNKS), 2, N_COPY)),
        pltpu.SemaphoreType.DMA((len(CHUNKS), 2, N_COPY)),
    ]
    for _, rows, z_first in CHUNKS:
        z = () if z_first else (NZ,)
        for _ in range(2):
            scratch += [
                pltpu.VMEM((NZ, 4, 4, rows, HALF) if z_first else (4, 4, NZ, rows, HALF), F32),
                pltpu.VMEM((2, 4, *z, rows // 2, HALF), F32),
                pltpu.VMEM((4, *z, rows, HALF), F32),
                pltpu.VMEM((4, *z, rows, HALF), F32),
                pltpu.VMEM((2, *z, rows // 2, HALF), F32),
                pltpu.VMEM((*z, rows, HALF), F32),
                pltpu.VMEM((*z, rows, HALF), F32),
                pltpu.VMEM((4, 4, rows, HALF) if z_first else (rows, HALF), F32),
            ]
    vmem = pl.BlockSpec(memory_space=pltpu.VMEM)
    return pl.pallas_call(
        kernel,
        out_shape=(
            jax.ShapeDtypeStruct((LR, RANK), F32),
            jax.ShapeDtypeStruct((1, LR, RANK), F32),
        ),
        in_specs=[pl.BlockSpec(memory_space=pl.ANY), vmem, vmem, vmem],
        out_specs=(vmem, vmem),
        scratch_shapes=scratch,
        compiler_params=pltpu.CompilerParams(
            collective_id=0, has_side_effects=True, vmem_limit_bytes=56 * 2**20
        ),
        name="bases",
    )(matrix, probes, skel, node_skel)


def on_device(matrix, probes, leaf_skeleton, node_skeleton):
    return bases(matrix, probes, leaf_skeleton, node_skeleton)


def solution(mesh):
    return jax.shard_map(
        on_device,
        mesh=mesh,
        in_specs=(P("grp", "leaf"), P("leaf", None), P(("grp", "leaf"), None), P()),
        out_specs=(P(("grp", "leaf"), None), P(("grp", "leaf"), None, None)),
        check_vma=False,
    )
```
